512 devices in a mesh: seq: 16 (over z_lo, core), chan: 32 (over x, z_hi, y).
Axes of the slice: x: 4, y: 4, z: 16 (z_hi: 2, z_lo: 8; z = z_hi * 8 + z_lo), core: 2. Of those that a mesh axis runs over, the one named last changes fastest.
Arguments:
- inner_gate: bfloat16 [2048, 8192], P('seq', 'chan'), may hold values from -6 to 6
- value_in: bfloat16 [2048, 8192], P('seq', 'chan'), may hold values from -6 to 6
- outer_gate: bfloat16 [2048, 8192], P('seq', 'chan'), may hold values from -6 to 6
- filter_taps: bfloat16 [2048, 8192], P('seq', 'chan'), may hold values from -5 to 5
- out_weight: bfloat16 [8192, 8192], P('chan'), may hold values from -0.125 to 0.125
Outputs:
- mixed: float32 [2048, 8192], P('seq', 'chan')
The draws below stay inside these ranges and needn't reach their ends.
All inputs are finite; a program needn't handle non-finite values.
Results may differ from the reference program's by a relative error of at most 0.0029.
Values may be sent and summed in bfloat16 or wider, within the bound.
A program may use at most 64 MiB of HBM per device.

```python
import math
import jax
import jax.numpy as jnp
from jax import lax

D = 8192
CH_DEV = 256
CHANNELS = 8192
TOKENS = 2048
N_CHAN = 32


def draw_filter_taps(key, part):
    key = jax.random.fold_in(key, 17)
    key_rate, key_noise = jax.random.split(key)
    lag = jnp.arange(TOKENS, dtype=jnp.float32)[:, None]
    decay_rate = jnp.exp(jax.random.uniform(key_rate, (1, CHANNELS), jnp.float32, math.log(0.25 / TOKENS), math.log(1.0 / 30.0)))
    roughness = jnp.clip(jax.random.normal(key_noise, (TOKENS, CHANNELS), jnp.float32), -4.0, 4.0)
    envelope = jnp.exp(-lag * decay_rate)
    energy = jnp.sqrt(jnp.expm1(-2.0 * decay_rate * TOKENS) / jnp.expm1(-2.0 * decay_rate))
    return (roughness * envelope / energy).astype(jnp.bfloat16)


def strengthened(values, own_key, source, target, blocks, factor):
    def block_of(dim):
        return (jnp.arange(values.shape[dim]) // (values.shape[dim] // blocks)).reshape((-1,) + (1,) * (values.ndim - 1 - dim))

    one_side = jax.random.permutation(own_key, blocks)[block_of(target)]
    other_side = (block_of(target) + blocks // 2) % blocks
    return jnp.where((block_of(source) == one_side) | (block_of(source) == other_side), factor * values, values)


def block_scale(stream_key, extent, pieces, least, largest):
    loudness, own = 1.0, jax.random.fold_in(stream_key, 6)
    for dim, shards_of in pieces:
        heights = jnp.exp(jax.random.uniform(jax.random.fold_in(own, dim), (shards_of,), jnp.float32, least / len(pieces), largest / len(pieces)))
        loudness = loudness * jnp.repeat(heights, extent[dim] // shards_of).reshape([-1 if axis == dim else 1 for axis in range(len(extent))])
    return loudness


def scatter_about(stream_key, shape, scale, most, shards=(), kind=jnp.bfloat16):
    level = block_scale(stream_key, shape, shards, -0.22, 0.18) if shards else 1.0
    result = jax.random.normal(stream_key, shape, jnp.float32) * scale * level
    return jnp.minimum(jnp.maximum(result, -most), most).astype(kind)


def gaussian_with(own_key, extent, deviation, bound, cuts, heavy, kind=jnp.bfloat16):
    values = deviation * jax.random.normal(own_key, extent, jnp.float32)
    if cuts:
        values = values * block_scale(own_key, extent, cuts, -0.22, 0.18)
    return jnp.clip(strengthened(values, jax.random.fold_in(own_key, 3), *heavy), -bound, bound).astype(kind)


def setup_inputs(seed: int = 0) -> dict:
    arg_keys = jax.random.split(jax.random.key(seed), 6)
    return {
        "inner_gate": scatter_about(arg_keys[0], (TOKENS, CHANNELS), 1.0, 6.0, ((0, 16), (1, 32))),
        "value_in": scatter_about(arg_keys[1], (TOKENS, CHANNELS), 1.0, 6.0, ((0, 16), (1, 32))),
        "outer_gate": scatter_about(arg_keys[2], (TOKENS, CHANNELS), 1.0, 6.0, ((0, 16), (1, 32))),
        "filter_taps": draw_filter_taps(jax.random.fold_in(arg_keys[5], 71), 0),
        "out_weight": gaussian_with(arg_keys[4], (CHANNELS, D), CHANNELS ** -0.5, 0.125, ((0, 32),), (0, 1, 32, 2.75)),
    }


def reference(inner_gate, value_in, outer_gate, filter_taps, out_weight):
    signal = inner_gate.astype(jnp.float32) * value_in.astype(jnp.float32)
    kernel = filter_taps.astype(jnp.float32)
    padded = 2 * TOKENS
    spectrum = jnp.fft.rfft(signal, n=padded, axis=0) * jnp.fft.rfft(kernel, n=padded, axis=0)
    convolved = jnp.fft.irfft(spectrum, n=padded, axis=0)[:TOKENS].astype(jnp.float32)
    gated = (outer_gate.astype(jnp.float32) * convolved).astype(jnp.bfloat16)

    def add_group(running, group_start):
        columns = lax.dynamic_slice_in_dim(gated, group_start, CH_DEV, 1)
        weight_rows = lax.dynamic_slice_in_dim(out_weight, group_start, CH_DEV, 0)
        partial_value = jnp.dot(columns, weight_rows, preferred_element_type=jnp.float32)
        return running + partial_value, None

    starts = (jnp.arange(N_CHAN, dtype=jnp.int32) * CH_DEV).astype(jnp.int32)
    running, unused = lax.scan(add_group, jnp.zeros((TOKENS, D), jnp.float32), starts)
    return running
```

```python
import functools

import jax
import jax.numpy as jnp
import ml_dtypes
import numpy as np
from jax import lax
from jax.experimental import pallas as pl
from jax.experimental.pallas import tpu as pltpu
from jax.sharding import PartitionSpec as P

MESH = pl.DeviceIdType.MESH
NX, NZ, NY = 4, 2, 4
F32, BF16 = jnp.float32, jnp.bfloat16


def split_bf16(values):
    high = values.astype(ml_dtypes.bfloat16)
    low = (values - high.astype(np.float64)).astype(ml_dtypes.bfloat16)
    return np.stack([high, low])


@functools.lru_cache(None)
def transform_constants(blocks, rows, group):
    j, b = np.arange(blocks), np.arange(rows)
    eye = np.eye(group)
    angle = 2 * np.pi * ((4 * j[:, None] + 1) * j[None, :] % (4 * blocks)) / (4 * blocks)
    f1 = np.concatenate([np.kron(np.cos(angle), eye), np.kron(-np.sin(angle), eye)], 0)
    f2 = np.concatenate([np.kron(np.cos(angle).T, eye), np.kron(np.sin(angle).T, eye)], 1) / (blocks * rows)
    turn = 2 * np.pi * ((4 * j[:, None] + 1) * b[None, :]) / (4 * blocks * rows)
    tw = np.stack([np.repeat(np.cos(turn), group, 0), np.repeat(np.sin(turn), group, 0)]).astype(np.float32)
    inner = 2 * np.pi * (b[:, None] * b[None, :] % rows) / rows
    c, s = np.cos(inner), np.sin(inner)
    g = np.block([[c, -s], [s, c]])
    return split_bf16(f1), split_bf16(f2), split_bf16(g), tw


def halves(value):
    high = value.astype(BF16)
    return high, (value - high.astype(F32)).astype(BF16)


def mm(a, b):
    return jnp.dot(a, b, preferred_element_type=F32)


def convolve(hi, lo, taps, f1, f2, g, tw):
    n, rows = hi.shape
    g_hi, g_lo = g[0], g[1]
    cos, sin = tw[0], tw[1]

    def within(re, im):
        high, low = halves(jnp.concatenate([re, im], 1))
        return mm(high, g_hi) + (mm(low, g_hi) + mm(high, g_lo))

    both = jnp.concatenate([hi, taps], 1)
    first = mm(f1[0], both) + mm(f1[1], both)
    sig = first[:, :rows] + mm(f1[0], lo)
    ker = first[:, rows:]

    def turned(re, im):
        return re * cos + im * sin, im * cos - re * sin

    s_re, s_im = turned(sig[:n], sig[n:])
    k_re, k_im = turned(ker[:n], ker[n:])
    spec = within(jnp.concatenate([s_re, k_re], 0), jnp.concatenate([s_im, k_im], 0))
    s_re, s_im = spec[:n, :rows], spec[:n, rows:]
    k_re, k_im = spec[n:, :rows], spec[n:, rows:]
    p_re = s_re * k_re - s_im * k_im
    p_im = -(s_re * k_im + s_im * k_re)
    back = within(p_re, p_im)
    w_re, w_im = turned(back[:, :rows], back[:, rows:])
    high, low = halves(jnp.concatenate([w_re, w_im], 0))
    out = mm(f2[0], jnp.concatenate([high, low], 1))
    return out[:, :rows] + (out[:, rows:] + mm(f2[1], high))


def kernel(
    inner_ref, value_ref, outer_ref, taps_ref, w_hbm, f1_hbm, f2_hbm, g_hbm, tw_hbm, out_ref,
    send, send_o, got, got_o, send_g, got_g, w, f1, f2, g, tw, acc, s1, r1, s2, r2, zs, zr,
    load_sem, a_ss, a_rs, o_ss, o_rs, g_ss, g_rs, s1_ss, s1_rs, s2_ss, s2_rs, z_ss, z_rs,
):
    seq = lax.axis_size("seq")
    me, chan = lax.axis_index("seq"), lax.axis_index("chan")
    x, zh, y = chan // (NZ * NY), chan // NY % NZ, chan % NY
    rows, channels = inner_ref.shape
    group = channels // seq
    half = rows // 2

    def at(dx, dz, dy):
        return ((x + dx) % NX * NZ + (zh + dz) % NZ) * NY + (y + dy) % NY

    loads = [
        pltpu.make_async_copy(src, dst, load_sem.at[i])
        for i, (src, dst) in enumerate([(f1_hbm, f1), (f2_hbm, f2), (g_hbm, g), (tw_hbm, tw), (w_hbm, w)])
    ]
    for load in loads:
        load.start()

    others = [(lax.rem(me + k, seq), chan) for k in range(1, seq)]
    others += [(me, at(d, 0, 0)) for d in range(1, NX)] + [(me, at(0, 0, d)) for d in range(1, NY)] + [(me, at(0, 1, 0))]
    barrier = pltpu.get_barrier_semaphore()
    for other in others:
        pl.semaphore_signal(barrier, inc=1, device_id=other, device_id_type=MESH)

    signal = (inner_ref[...].astype(F32) * value_ref[...].astype(F32)).T
    hi, lo = halves(signal)
    send[:, 0:group] = hi.reshape(seq, group, rows)
    send[:, group : 2 * group] = lo.reshape(seq, group, rows)
    send[:, 2 * group : 3 * group] = taps_ref[...].astype(F32).T.astype(BF16).reshape(seq, group, rows)
    send_o[...] = outer_ref[...].astype(F32).T.astype(BF16).reshape(seq, group, rows)
    pl.semaphore_wait(barrier, len(others))

    def spread(src, dst, ss, rs):
        copies = []
        for k in range(1, seq):
            to = lax.rem(me + k, seq)
            copy = pltpu.make_async_remote_copy(
                src_ref=src.at[to], dst_ref=dst.at[me], send_sem=ss.at[k - 1], recv_sem=rs.at[k - 1],
                device_id=(to, chan), device_id_type=MESH,
            )
            copy.start()
            copies.append(copy)
        return copies

    out_a = spread(send, got, a_ss, a_rs)
    out_o = spread(send_o, got_o, o_ss, o_rs)
    got[me] = send[me]
    got_o[me] = send_o[me]
    for load in loads[:4]:
        load.wait()
    for copy in out_a:
        copy.wait_recv()
    n = seq * group
    conv = convolve(
        got[:, 0:group].reshape(n, rows), got[:, group : 2 * group].reshape(n, rows),
        got[:, 2 * group : 3 * group].reshape(n, rows), f1, f2, g, tw,
    )
    for copy in out_o:
        copy.wait_recv()
    gated = (got_o[...].reshape(n, rows).astype(F32) * conv).astype(BF16)
    send_g[...] = gated.reshape(seq, group, rows)
    out_g = spread(send_g, got_g, g_ss, g_rs)
    got_g[me] = send_g[me]
    loads[4].wait()
    for copy in out_g:
        copy.wait_recv()
    mine = got_g[...].reshape(n, rows).astype(F32).T.astype(BF16)

    width = channels

    def remote(src, dst, ss, rs, dx, dz, dy):
        copy = pltpu.make_async_remote_copy(
            src_ref=src, dst_ref=dst, send_sem=ss, recv_sem=rs, device_id=(me, at(dx, dz, dy)), device_id_type=MESH
        )
        copy.start()
        return copy

    order = [2, 1, 3, 0]
    sent = []
    stage1 = {}
    for wave in range(2):
        dz = 1 - wave
        done = set()
        for first in order:
            todo = [(first, d) for d in order] + [(d, first) for d in order]
            for dx, dy in todo:
                if (dx, dy) in done:
                    continue
                done.add((dx, dy))
                column = pl.multiple_of(at(dx, dz, dy) * width, width)
                block = mm(mine, w[:, pl.ds(column, width)])
                if dx == 0:
                    acc[wave, 0, :, dy * width : (dy + 1) * width] = block[:half]
                else:
                    s1[wave, 0, dx - 1, :, dy * width : (dy + 1) * width] = block[:half].astype(BF16)
                if dy == 0:
                    acc[wave, 1, :, dx * width : (dx + 1) * width] = block[half:]
                else:
                    s1[wave, 1, dy - 1, :, dx * width : (dx + 1) * width] = block[half:].astype(BF16)
            if first:
                for h in range(2):
                    stage1[wave, h, first] = remote(
                        s1.at[wave, h, first - 1], r1.at[wave, h, first - 1],
                        s1_ss.at[wave, h, first - 1], s1_rs.at[wave, h, first - 1],
                        first * (1 - h), 0, first * h,
                    )
    last = []
    for wave in range(2):
        stage2 = {}
        for h in range(2):
            for d in (1, 3, 2):
                stage1[wave, h, d].wait_recv()
            for d in order:
                cols = slice(d * width, (d + 1) * width)
                total = acc[wave, h, :, cols]
                for e in range(3):
                    total = total + r1[wave, h, e, :, cols].astype(F32)
                if d:
                    s2[wave, h, d - 1] = total.astype(BF16)
                    stage2[h, d] = remote(
                        s2.at[wave, h, d - 1], r2.at[wave, h, d - 1],
                        s2_ss.at[wave, h, d - 1], s2_rs.at[wave, h, d - 1], d * h, 0, d * (1 - h),
                    )
                else:
                    acc[wave, h, :, cols] = total
        sent += list(stage2.values())
        for h in range(2):
            total = acc[wave, h, :, 0:width]
            for d in (1, 3, 2):
                stage2[h, d].wait_recv()
                total = total + r2[wave, h, d - 1].astype(F32)
            if wave == 0:
                zs[h] = total.astype(BF16)
                last.append(remote(zs.at[h], zr.at[h], z_ss.at[h], z_rs.at[h], 0, 1, 0))
            else:
                last[h].wait_recv()
                out_ref[h * half : (h + 1) * half, :] = total + zr[h].astype(F32)
    for copy in out_a + out_o + out_g + list(stage1.values()) + sent + last:
        copy.wait_send()


def local(inner_gate, value_in, outer_gate, filter_taps, out_weight):
    rows, channels = inner_gate.shape
    seq = lax.axis_size("seq")
    group, half = channels // seq, rows // 2
    f1, f2, g, tw = transform_constants(seq, rows, group)
    vmem, dma = pltpu.VMEM, pltpu.SemaphoreType.DMA
    in_vmem = pl.BlockSpec(memory_space=pltpu.VMEM)
    in_any = pl.BlockSpec(memory_space=pl.ANY)
    peers = seq - 1
    scratch = [
        vmem((seq, 3 * group, rows), BF16), vmem((seq, group, rows), BF16),
        vmem((seq, 3 * group, rows), BF16), vmem((seq, group, rows), BF16),
        vmem((seq, group, rows), BF16), vmem((seq, group, rows), BF16),
        vmem(out_weight.shape, BF16), vmem(f1.shape, BF16), vmem(f2.shape, BF16), vmem(g.shape, BF16), vmem(tw.shape, F32),
        vmem((2, 2, half, 4 * channels), F32),
        vmem((2, 2, 3, half, 4 * channels), BF16), vmem((2, 2, 3, half, 4 * channels), BF16),
        vmem((2, 2, 3, half, channels), BF16), vmem((2, 2, 3, half, channels), BF16),
        vmem((2, half, channels), BF16), vmem((2, half, channels), BF16),
        dma((5,)), dma((peers,)), dma((peers,)), dma((peers,)), dma((peers,)), dma((peers,)), dma((peers,)),
        dma((2, 2, 3)), dma((2, 2, 3)), dma((2, 2, 3)), dma((2, 2, 3)), dma((2,)), dma((2,)),
    ]
    return pl.pallas_call(
        kernel,
        out_shape=jax.ShapeDtypeStruct((rows, channels), F32),
        in_specs=[in_vmem] * 4 + [in_any] * 5,
        out_specs=in_vmem,
        scratch_shapes=scratch,
        compiler_params=pltpu.CompilerParams(collective_id=0, has_side_effects=True, vmem_limit_bytes=48 * 2**20),
        name="hyena",
    )(inner_gate, value_in, outer_gate, filter_taps, out_weight, *(jnp.asarray(c) for c in (f1, f2, g, tw)))


def solution(mesh):
    in_specs = (P("seq", "chan"),) * 4 + (P("chan", None),)
    return jax.shard_map(local, mesh=mesh, in_specs=in_specs, out_specs=P("seq", "chan"), check_vma=False)
```

```python
import functools

import jax
import jax.numpy as jnp
import ml_dtypes
import numpy as np
from jax import lax
from jax.experimental import pallas as pl
from jax.experimental.pallas import tpu as pltpu
from jax.sharding import PartitionSpec as P

MESH = pl.DeviceIdType.MESH
NX, NZ, NY = 4, 2, 4
F32, BF16 = jnp.float32, jnp.bfloat16


def split_bf16(values):
    high = values.astype(ml_dtypes.bfloat16)
    low = (values - high.astype(np.float64)).astype(ml_dtypes.bfloat16)
    return np.stack([high, low])


@functools.lru_cache(None)
def transform_constants(blocks, rows, group):
    j, b = np.arange(blocks), np.arange(rows)
    eye = np.eye(group)
    angle = 2 * np.pi * ((4 * j[:, None] + 1) * j[None, :] % (4 * blocks)) / (4 * blocks)
    f1 = np.concatenate([np.kron(np.cos(angle), eye), np.kron(-np.sin(angle), eye)], 0)
    f2 = np.concatenate([np.kron(np.cos(angle).T, eye), np.kron(np.sin(angle).T, eye)], 1) / (blocks * rows)
    turn = 2 * np.pi * ((4 * j[:, None] + 1) * b[None, :]) / (4 * blocks * rows)
    tw = np.stack([np.repeat(np.cos(turn), group, 0), np.repeat(np.sin(turn), group, 0)]).astype(np.float32)
    inner = 2 * np.pi * (b[:, None] * b[None, :] % rows) / rows
    c, s = np.cos(inner), np.sin(inner)
    g = np.block([[c, -s], [s, c]])
    return split_bf16(f1), split_bf16(f2), split_bf16(g), tw


def halves(value):
    high = value.astype(BF16)
    return high, (value - high.astype(F32)).astype(BF16)


def mm(a, b):
    return jnp.dot(a, b, preferred_element_type=F32)


def convolve(hi, lo, taps, f1, f2, g, tw):
    n, rows = hi.shape
    g_hi, g_lo = g[0], g[1]
    cos, sin = tw[0], tw[1]

    def within(re, im):
        high, low = halves(jnp.concatenate([re, im], 1))
        return mm(high, g_hi) + (mm(low, g_hi) + mm(high, g_lo))

    both = jnp.concatenate([hi, taps], 1)
    first = mm(f1[0], both) + mm(f1[1], both)
    sig = first[:, :rows] + mm(f1[0], lo)
    ker = first[:, rows:]

    def turned(re, im):
        return re * cos + im * sin, im * cos - re * sin

    s_re, s_im = turned(sig[:n], sig[n:])
    k_re, k_im = turned(ker[:n], ker[n:])
    spec = within(jnp.concatenate([s_re, k_re], 0), jnp.concatenate([s_im, k_im], 0))
    s_re, s_im = spec[:n, :rows], spec[:n, rows:]
    k_re, k_im = spec[n:, :rows], spec[n:, rows:]
    p_re = s_re * k_re - s_im * k_im
    p_im = -(s_re * k_im + s_im * k_re)
    back = within(p_re, p_im)
    w_re, w_im = turned(back[:, :rows], back[:, rows:])
    high, low = halves(jnp.concatenate([w_re, w_im], 0))
    out = mm(f2[0], jnp.concatenate([high, low], 1))
    return out[:, :rows] + (out[:, rows:] + mm(f2[1], high))


def kernel(
    inner_hbm, value_hbm, outer_hbm, taps_hbm, w_hbm, f1_hbm, f2_hbm, g_hbm, tw_hbm, own_hbm, far_hbm,
    inner_ref, value_ref, outer_ref, taps_ref, send, send_o, got, got_o, send_g, got_g, w, f1, f2, g, tw, acc, s1, r1, s2, r2, zs, own,
    load_sem, own_sem, far_sem, a_ss, a_rs, o_ss, o_rs, g_ss, g_rs, s1_ss, s1_rs, s2_ss, s2_rs, z_ss, z_rs,
):
    seq = lax.axis_size("seq")
    me, chan = lax.axis_index("seq"), lax.axis_index("chan")
    x, zh, y = chan // (NZ * NY), chan // NY % NZ, chan % NY
    rows, channels = own_hbm.shape
    group = channels // seq
    half = rows // 2

    def at(dx, dz, dy):
        return ((x + dx) % NX * NZ + (zh + dz) % NZ) * NY + (y + dy) % NY

    others = [(lax.rem(me + k, seq), chan) for k in range(1, seq)]
    others += [(me, at(d, 0, 0)) for d in range(1, NX)] + [(me, at(0, 0, d)) for d in range(1, NY)]
    barrier = pltpu.get_barrier_semaphore()
    for other in others:
        pl.semaphore_signal(barrier, inc=1, device_id=other, device_id_type=MESH)
    far = (me, at(0, 1, 0))

    @pl.when(zh == 0)
    def _():
        pl.semaphore_signal(barrier, inc=1, device_id=far, device_id_type=MESH)

    pairs = [
        (inner_hbm, inner_ref), (value_hbm, value_ref), (taps_hbm, taps_ref), (outer_hbm, outer_ref),
        (f1_hbm, f1), (f2_hbm, f2), (g_hbm, g), (tw_hbm, tw), (w_hbm, w),
    ]
    loads = [pltpu.make_async_copy(src, dst, load_sem.at[i]) for i, (src, dst) in enumerate(pairs)]
    for load in loads:
        load.start()

    loads[0].wait()
    loads[1].wait()
    signal = (inner_ref[...].astype(F32) * value_ref[...].astype(F32)).T
    hi, lo = halves(signal)
    send[:, 0:group] = hi.reshape(seq, group, rows)
    send[:, group : 2 * group] = lo.reshape(seq, group, rows)
    loads[2].wait()
    send[:, 2 * group : 3 * group] = taps_ref[...].astype(F32).T.astype(BF16).reshape(seq, group, rows)
    loads[3].wait()
    send_o[...] = outer_ref[...].astype(F32).T.astype(BF16).reshape(seq, group, rows)
    pl.semaphore_wait(barrier, len(others) + zh)

    @pl.when(zh == 1)
    def _():
        pl.semaphore_signal(far_sem, inc=1, device_id=far, device_id_type=MESH)

    def spread(src, dst, ss, rs):
        copies = []
        for k in range(1, seq):
            to = lax.rem(me + k, seq)
            copy = pltpu.make_async_remote_copy(
                src_ref=src.at[to], dst_ref=dst.at[me], send_sem=ss.at[k - 1], recv_sem=rs.at[k - 1],
                device_id=(to, chan), device_id_type=MESH,
            )
            copy.start()
            copies.append(copy)
        return copies

    out_a = spread(send, got, a_ss, a_rs)
    out_o = spread(send_o, got_o, o_ss, o_rs)
    got[me] = send[me]
    got_o[me] = send_o[me]
    for load in loads[4:8]:
        load.wait()
    for copy in out_a:
        copy.wait_recv()
    n = seq * group
    conv = convolve(
        got[:, 0:group].reshape(n, rows), got[:, group : 2 * group].reshape(n, rows),
        got[:, 2 * group : 3 * group].reshape(n, rows), f1, f2, g, tw,
    )
    for copy in out_o:
        copy.wait_recv()
    gated = (got_o[...].reshape(n, rows).astype(F32) * conv).astype(BF16)
    send_g[...] = gated.reshape(seq, group, rows)
    out_g = []
    for i in range(seq - 1):
        to = i + (i >= me).astype(jnp.int32)
        copy = pltpu.make_async_remote_copy(
            src_ref=send_g.at[to], dst_ref=got_g.at[me], send_sem=g_ss.at[to], recv_sem=g_rs.at[me],
            device_id=(to, chan), device_id_type=MESH,
        )
        copy.start()
        out_g.append(copy)
    got_g[me] = send_g[me]
    loads[8].wait()
    for i in range(seq - 1):
        other = i + (i >= me).astype(jnp.int32)
        pltpu.make_async_remote_copy(
            src_ref=send_g.at[other], dst_ref=got_g.at[other], send_sem=g_ss.at[other], recv_sem=g_rs.at[other],
            device_id=(other, chan), device_id_type=MESH,
        ).wait_recv()
    mine = got_g[...].reshape(n, rows).astype(F32).T.astype(BF16)

    width = channels

    def remote(src, dst, ss, rs, dx, dz, dy):
        copy = pltpu.make_async_remote_copy(
            src_ref=src, dst_ref=dst, send_sem=ss, recv_sem=rs, device_id=(me, at(dx, dz, dy)), device_id_type=MESH
        )
        copy.start()
        return copy

    order = [2, 1, 3, 0]

    def start1(wave, h, d):
        stage1[wave, h, d] = remote(
            s1.at[wave, h, d - 1], r1.at[wave, h, d - 1], s1_ss.at[wave, h, d - 1], s1_rs.at[wave, h, d - 1],
            d * (1 - h), 0, d * h,
        )

    sent = []
    stage1 = {}
    for wave in range(2):
        dz = 1 - wave
        done = set()
        for first in order:
            todo = [(first, d) for d in order] + [(d, first) for d in order]
            for dx, dy in todo:
                if (dx, dy) in done:
                    continue
                done.add((dx, dy))
                column = pl.multiple_of(at(dx, dz, dy) * width, width)
                block = mm(mine, w[:, pl.ds(column, width)])
                if dx == 0:
                    acc[wave, 0, :, dy * width : (dy + 1) * width] = block[:half]
                else:
                    s1[wave, 0, dx - 1, :, dy * width : (dy + 1) * width] = block[:half].astype(BF16)
                if dy == 0:
                    acc[wave, 1, :, dx * width : (dx + 1) * width] = block[half:]
                else:
                    s1[wave, 1, dy - 1, :, dx * width : (dx + 1) * width] = block[half:].astype(BF16)
            if first and wave == 0:
                for h in range(2):
                    start1(wave, h, first)
    last = []
    for wave in range(2):
        stage2 = {}
        for h in range(2):
            for d in (1, 3, 2):
                stage1[wave, h, d].wait_recv()
            for d in order:
                cols = slice(d * width, (d + 1) * width)
                total = acc[wave, h, :, cols]
                for e in range(3):
                    total = total + r1[wave, h, e, :, cols].astype(F32)
                if d:
                    s2[wave, h, d - 1] = total.astype(BF16)
                    stage2[h, d] = remote(
                        s2.at[wave, h, d - 1], r2.at[wave, h, d - 1],
                        s2_ss.at[wave, h, d - 1], s2_rs.at[wave, h, d - 1], d * h, 0, d * (1 - h),
                    )
                else:
                    acc[wave, h, :, cols] = total
        sent += list(stage2.values())
        if wave == 0:
            for d in order[:3]:
                for h in range(2):
                    start1(1, h, d)
        for h in range(2):
            total = acc[wave, h, :, 0:width]
            for d in (1, 3, 2):
                stage2[h, d].wait_recv()
                total = total + r2[wave, h, d - 1].astype(F32)
            if wave == 0:
                if h == 0:

                    @pl.when(zh == 0)
                    def _():
                        pl.semaphore_wait(far_sem, 1)

                zs[h] = total.astype(BF16)
                last.append(remote(zs.at[h], far_hbm.at[h], z_ss.at[h], z_rs.at[h], 0, 1, 0))
            else:
                own[h * half : (h + 1) * half] = total
    store = pltpu.make_async_copy(own, own_hbm, own_sem)
    store.start()
    for copy in last:
        copy.wait_recv()
    store.wait()
    for copy in out_a + out_o + out_g + list(stage1.values()) + sent + last:
        copy.wait_send()


def local(inner_gate, value_in, outer_gate, filter_taps, out_weight):
    rows, channels = inner_gate.shape
    seq = lax.axis_size("seq")
    group, half = channels // seq, rows // 2
    f1, f2, g, tw = transform_constants(seq, rows, group)
    vmem, dma = pltpu.VMEM, pltpu.SemaphoreType.DMA
    in_hbm = pl.BlockSpec(memory_space=pltpu.HBM)
    peers = seq - 1
    scratch = [
        *[vmem((rows, channels), BF16)] * 4,
        vmem((seq, 3 * group, rows), BF16), vmem((seq, group, rows), BF16),
        vmem((seq, 3 * group, rows), BF16), vmem((seq, group, rows), BF16),
        vmem((seq, group, rows), BF16), vmem((seq, group, rows), BF16),
        vmem(out_weight.shape, BF16), vmem(f1.shape, BF16), vmem(f2.shape, BF16), vmem(g.shape, BF16), vmem(tw.shape, F32),
        vmem((2, 2, half, 4 * channels), F32),
        vmem((2, 2, 3, half, 4 * channels), BF16), vmem((2, 2, 3, half, 4 * channels), BF16),
        vmem((2, 2, 3, half, channels), BF16), vmem((2, 2, 3, half, channels), BF16),
        vmem((2, half, channels), BF16), vmem((rows, channels), F32),
        dma((9,)), dma(()), pltpu.SemaphoreType.REGULAR, dma((peers,)), dma((peers,)), dma((peers,)), dma((peers,)), dma((seq,)), dma((seq,)),
        dma((2, 2, 3)), dma((2, 2, 3)), dma((2, 2, 3)), dma((2, 2, 3)), dma((2,)), dma((2,)),
    ]
    own, far = pl.pallas_call(
        kernel,
        out_shape=(jax.ShapeDtypeStruct((rows, channels), F32), jax.ShapeDtypeStruct((2, half, channels), BF16)),
        in_specs=[in_hbm] * 9,
        out_specs=(in_hbm, in_hbm),
        scratch_shapes=scratch,
        compiler_params=pltpu.CompilerParams(collective_id=0, has_side_effects=True, vmem_limit_bytes=62 * 2**20),
        name="hyena",
    )(inner_gate, value_in, outer_gate, filter_taps, out_weight, *(jnp.asarray(c) for c in (f1, f2, g, tw)))
    return own + far.reshape(rows, channels).astype(F32)


def solution(mesh):
    in_specs = (P("seq", "chan"),) * 4 + (P("chan", None),)
    return jax.shard_map(local, mesh=mesh, in_specs=in_specs, out_specs=P("seq", "chan"), check_vma=False)
```

```python
import functools

import jax
import jax.numpy as jnp
import ml_dtypes
import numpy as np
from jax import lax
from jax.experimental import pallas as pl
from jax.experimental.pallas import tpu as pltpu
from jax.sharding import PartitionSpec as P

MESH = pl.DeviceIdType.MESH
NX, NZ, NY = 4, 2, 4
F32, BF16 = jnp.float32, jnp.bfloat16


def split_bf16(values):
    high = values.astype(ml_dtypes.bfloat16)
    low = (values - high.astype(np.float64)).astype(ml_dtypes.bfloat16)
    return np.stack([high, low])


@functools.lru_cache(None)
def transform_constants(blocks, rows, group):
    j, b = np.arange(blocks), np.arange(rows)
    eye = np.eye(group)
    angle = 2 * np.pi * ((4 * j[:, None] + 1) * j[None, :] % (4 * blocks)) / (4 * blocks)
    f1 = np.concatenate([np.kron(np.cos(angle), eye), np.kron(-np.sin(angle), eye)], 0)
    f2 = np.concatenate([np.kron(np.cos(angle).T, eye), np.kron(np.sin(angle).T, eye)], 1) / (blocks * rows)
    turn = 2 * np.pi * ((4 * j[:, None] + 1) * b[None, :]) / (4 * blocks * rows)
    tw = np.stack([np.repeat(np.cos(turn), group, 0), np.repeat(np.sin(turn), group, 0)]).astype(np.float32)
    inner = 2 * np.pi * (b[:, None] * b[None, :] % rows) / rows
    c, s = np.cos(inner), np.sin(inner)
    g = np.block([[c, -s], [s, c]])
    return split_bf16(f1), split_bf16(f2), split_bf16(g), tw


def halves(value):
    high = value.astype(BF16)
    return high, (value - high.astype(F32)).astype(BF16)


def mm(a, b):
    return jnp.dot(a, b, preferred_element_type=F32)


def convolve(hi, lo, taps, f1, f2, g, tw):
    n, rows = hi.shape
    g_hi, g_lo = g[0], g[1]
    cos, sin = tw[0], tw[1]

    def within(re, im):
        high, low = halves(jnp.concatenate([re, im], 1))
        return mm(high, g_hi) + (mm(low, g_hi) + mm(high, g_lo))

    both = jnp.concatenate([hi, taps], 1)
    first = mm(f1[0], both) + mm(f1[1], both)
    sig = first[:, :rows] + mm(f1[0], lo)
    ker = first[:, rows:]

    def turned(re, im):
        return re * cos + im * sin, im * cos - re * sin

    s_re, s_im = turned(sig[:n], sig[n:])
    k_re, k_im = turned(ker[:n], ker[n:])
    spec = within(jnp.concatenate([s_re, k_re], 0), jnp.concatenate([s_im, k_im], 0))
    s_re, s_im = spec[:n, :rows], spec[:n, rows:]
    k_re, k_im = spec[n:, :rows], spec[n:, rows:]
    p_re = s_re * k_re - s_im * k_im
    p_im = -(s_re * k_im + s_im * k_re)
    back = within(p_re, p_im)
    w_re, w_im = turned(back[:, :rows], back[:, rows:])
    high, low = halves(jnp.concatenate([w_re, w_im], 0))
    out = mm(f2[0], jnp.concatenate([high, low], 1))
    return out[:, :rows] + (out[:, rows:] + mm(f2[1], high))


def kernel(
    inner_hbm, value_hbm, outer_hbm, taps_hbm, w_hbm, f1_hbm, f2_hbm, g_hbm, tw_hbm, own_hbm, far_hbm,
    inner_ref, value_ref, outer_ref, taps_ref, send, send_o, got, got_o, send_g, got_g, w, wxa, wxb, f1, f2, g, tw, mine, gx, acc0, acc1, s1, r1, s2, r2, zs, own,
    load_sem, own_sem, far_sem, a_ss, a_rs, o_ss, o_rs, g_ss, g_rs, wa_ss, wa_rs, wb_ss, wb_rs, f_ss, f_rs, gx_ss, gx_rs, s1_ss, s1_rs, s2_ss, s2_rs, z_ss, z_rs,
):
    seq = lax.axis_size("seq")
    me, chan = lax.axis_index("seq"), lax.axis_index("chan")
    x, zh, y = chan // (NZ * NY), chan // NY % NZ, chan % NY
    rows, channels = own_hbm.shape
    group = channels // seq
    half = rows // 2

    def at(dx, dz, dy):
        return ((x + dx) % NX * NZ + (zh + dz) % NZ) * NY + (y + dy) % NY

    others = [(lax.rem(me + k, seq), chan) for k in range(1, seq)]
    others += [(me, at(d, 0, 0)) for d in range(1, NX)] + [(me, at(0, 0, d)) for d in range(1, NY)]
    barrier = pltpu.get_barrier_semaphore()
    for other in others:
        pl.semaphore_signal(barrier, inc=1, device_id=other, device_id_type=MESH)
    far = (me, at(0, 1, 0))

    @pl.when(zh == 0)
    def _():
        pl.semaphore_signal(barrier, inc=1, device_id=far, device_id_type=MESH)

    pairs = [
        (inner_hbm, inner_ref), (value_hbm, value_ref), (taps_hbm, taps_ref), (outer_hbm, outer_ref),
        (f1_hbm, f1), (f2_hbm, f2), (g_hbm, g), (tw_hbm, tw), (w_hbm, w),
    ]
    loads = [pltpu.make_async_copy(src, dst, load_sem.at[i]) for i, (src, dst) in enumerate(pairs)]
    for load in loads:
        load.start()

    loads[0].wait()
    loads[1].wait()
    signal = (inner_ref[...].astype(F32) * value_ref[...].astype(F32)).T
    hi, lo = halves(signal)
    send[:, 0:group] = hi.reshape(seq, group, rows)
    send[:, group : 2 * group] = lo.reshape(seq, group, rows)
    loads[2].wait()
    send[:, 2 * group : 3 * group] = taps_ref[...].astype(F32).T.astype(BF16).reshape(seq, group, rows)
    loads[3].wait()
    send_o[...] = outer_ref[...].astype(F32).T.astype(BF16).reshape(seq, group, rows)
    pl.semaphore_wait(barrier, len(others) + zh)

    @pl.when(zh == 1)
    def _():
        pl.semaphore_signal(far_sem, inc=1, device_id=far, device_id_type=MESH)

    def spread(src, dst, ss, rs):
        copies = []
        for k in range(1, seq):
            to = lax.rem(me + k, seq)
            copy = pltpu.make_async_remote_copy(
                src_ref=src.at[to], dst_ref=dst.at[me], send_sem=ss.at[k - 1], recv_sem=rs.at[k - 1],
                device_id=(to, chan), device_id_type=MESH,
            )
            copy.start()
            copies.append(copy)
        return copies

    def remote(src, dst, ss, rs, dx=0, dz=0, dy=0, to=None):
        copy = pltpu.make_async_remote_copy(
            src_ref=src, dst_ref=dst, send_sem=ss, recv_sem=rs,
            device_id=(me, at(dx, dz, dy)) if to is None else to, device_id_type=MESH,
        )
        copy.start()
        return copy

    out_a = spread(send, got, a_ss, a_rs)
    out_o = spread(send_o, got_o, o_ss, o_rs)
    order, width = [2, 1, 3, 0], channels
    core = lax.rem(me, 2)
    sibling = (me + 1 - 2 * core, chan)
    part = pl.ds(pl.multiple_of(core * (channels // 2), channels // 2), channels // 2)
    weights, onward = {}, []
    loads[8].wait()
    for d in order[:3]:
        column = pl.multiple_of(((x + d) % NX * NZ + 1 - zh) * NY * width, NY * width)
        weights[0, d] = remote(
            w.at[part, pl.ds(column, NY * width)], wxa.at[d - 1, part], wa_ss.at[d - 1], wa_rs.at[d - 1], dx=d
        )
        for i in range(NX):
            column = pl.multiple_of(((i * NZ + 1 - zh) * NY + (y + d) % NY) * width, width)
            weights[1, d, i] = remote(
                w.at[part, pl.ds(column, width)], wxb.at[d - 1, i, part], wb_ss.at[d - 1, i], wb_rs.at[d - 1, i], dy=d
            )
    got[me] = send[me]
    got_o[me] = send_o[me]
    for load in loads[4:8]:
        load.wait()
    for copy in out_a:
        copy.wait_recv()
    n = seq * group
    conv = convolve(
        got[:, 0:group].reshape(n, rows), got[:, group : 2 * group].reshape(n, rows),
        got[:, 2 * group : 3 * group].reshape(n, rows), f1, f2, g, tw,
    )
    for copy in out_o:
        copy.wait_recv()
    gated = (got_o[...].reshape(n, rows).astype(F32) * conv).astype(BF16)
    send_g[...] = gated.reshape(seq, group, rows)
    out_g = []
    for i in range(seq - 1):
        to = i + (i >= me).astype(jnp.int32)
        copy = pltpu.make_async_remote_copy(
            src_ref=send_g.at[to], dst_ref=got_g.at[me], send_sem=g_ss.at[to], recv_sem=g_rs.at[me],
            device_id=(to, chan), device_id_type=MESH,
        )
        copy.start()
        out_g.append(copy)
    got_g[me] = send_g[me]
    for d in order:
        if d:
            weights[0, d].wait_recv()
            onward.append(remote(wxa.at[d - 1, part], wxa.at[d - 1, part], f_ss.at[0, d - 1], f_rs.at[0, d - 1], to=sibling))
            for i in range(NX):
                weights[1, d, i].wait_recv()
            onward.append(remote(wxb.at[d - 1, :, part], wxb.at[d - 1, :, part], f_ss.at[1, d - 1], f_rs.at[1, d - 1], to=sibling))
    for i in range(seq - 1):
        other = i + (i >= me).astype(jnp.int32)
        pltpu.make_async_remote_copy(
            src_ref=send_g.at[other], dst_ref=got_g.at[other], send_sem=g_ss.at[other], recv_sem=g_rs.at[other],
            device_id=(other, chan), device_id_type=MESH,
        ).wait_recv()
    mine[...] = got_g[...].reshape(n, rows).astype(F32).T.astype(BF16)

    gather, stage1, stage2, last = {}, {}, {}, []
    for d in order[:3]:
        for h in range(2):
            gather[h, d] = remote(
                mine.at[pl.ds(h * half, half)], gx.at[h, d - 1], gx_ss.at[h, d - 1], gx_rs.at[h, d - 1],
                d * (1 - h), 0, d * h,
            )
    for i in range(4):
        for h in range(2):
            block = (x * NZ + 1 - zh) * NY + i if h == 0 else (i * NZ + 1 - zh) * NY + y
            column = pl.multiple_of(block * width, width)
            acc0[h, i] = mm(mine[h * half : (h + 1) * half], w[:, pl.ds(column, width)])
    for dx in order:
        for dy in order:
            column = pl.multiple_of(at(dx, 0, dy) * width, width)
            block = mm(mine[...], w[:, pl.ds(column, width)])
            if dx == 0:
                acc1[0, dy] = block[:half]
            else:
                s1[0, dx - 1, :, dy * width : (dy + 1) * width] = block[:half].astype(BF16)
            if dy == 0:
                acc1[1, dx] = block[half:]
            else:
                s1[1, dy - 1, :, dx * width : (dx + 1) * width] = block[half:].astype(BF16)
    for copy in onward:
        copy.wait_recv()
    for d in (1, 3, 2):
        for h in range(2):
            gather[h, d].wait_recv()
            for i in range(4):
                block = wxa[d - 1, :, i * width : (i + 1) * width] if h == 0 else wxb[d - 1, i]
                acc0[h, i] += mm(gx[h, d - 1], block)

    def second(wave, h, d, total):
        s2[wave, h, d - 1] = total.astype(BF16)
        stage2[wave, h, d] = remote(
            s2.at[wave, h, d - 1], r2.at[wave, h, d - 1], s2_ss.at[wave, h, d - 1], s2_rs.at[wave, h, d - 1],
            d * h, 0, d * (1 - h),
        )

    def finished(wave, h, total):
        for d in (1, 3, 2):
            stage2[wave, h, d].wait_recv()
            total = total + r2[wave, h, d - 1].astype(F32)
        return total

    for d in order[:3]:
        for h in range(2):
            second(0, h, d, acc0[h, (y + d) % NY if h == 0 else (x + d) % NX])
    for d in order[:3]:
        for h in range(2):
            stage1[h, d] = remote(
                s1.at[h, d - 1], r1.at[h, d - 1], s1_ss.at[h, d - 1], s1_rs.at[h, d - 1], d * (1 - h), 0, d * h
            )
    for h in range(2):
        total = finished(0, h, acc0[h, y if h == 0 else x])
        if h == 0:

            @pl.when(zh == 0)
            def _():
                pl.semaphore_wait(far_sem, 1)

        zs[h] = total.astype(BF16)
        last.append(remote(zs.at[h], far_hbm.at[h], z_ss.at[h], z_rs.at[h], 0, 1, 0))
    for h in range(2):
        for d in (1, 3, 2):
            stage1[h, d].wait_recv()
        for d in order:
            total = acc1[h, d]
            for e in range(3):
                total = total + r1[h, e, :, d * width : (d + 1) * width].astype(F32)
            if d:
                second(1, h, d, total)
            else:
                acc1[h, 0] = total
    for h in range(2):
        own[h * half : (h + 1) * half] = finished(1, h, acc1[h, 0])
    store = pltpu.make_async_copy(own, own_hbm, own_sem)
    store.start()
    for copy in last:
        copy.wait_recv()
    store.wait()
    groups = (weights, gather, stage1, stage2)
    for copy in out_a + out_o + out_g + onward + last + [copy for g in groups for copy in g.values()]:
        copy.wait_send()


def local(inner_gate, value_in, outer_gate, filter_taps, out_weight):
    rows, channels = inner_gate.shape
    seq = lax.axis_size("seq")
    group, half = channels // seq, rows // 2
    f1, f2, g, tw = transform_constants(seq, rows, group)
    vmem, dma = pltpu.VMEM, pltpu.SemaphoreType.DMA
    in_hbm = pl.BlockSpec(memory_space=pltpu.HBM)
    peers = seq - 1
    scratch = [
        *[vmem((rows, channels), BF16)] * 4,
        vmem((seq, 3 * group, rows), BF16), vmem((seq, group, rows), BF16),
        vmem((seq, 3 * group, rows), BF16), vmem((seq, group, rows), BF16),
        vmem((seq, group, rows), BF16), vmem((seq, group, rows), BF16),
        vmem(out_weight.shape, BF16), vmem((3, channels, NY * channels), BF16), vmem((3, NX, channels, channels), BF16),
        vmem(f1.shape, BF16), vmem(f2.shape, BF16), vmem(g.shape, BF16), vmem(tw.shape, F32),
        vmem((rows, channels), BF16), vmem((2, 3, half, channels), BF16),
        vmem((2, 4, half, channels), F32), vmem((2, 4, half, channels), F32),
        vmem((2, 3, half, 4 * channels), BF16), vmem((2, 3, half, 4 * channels), BF16),
        vmem((2, 2, 3, half, channels), BF16), vmem((2, 2, 3, half, channels), BF16),
        vmem((2, half, channels), BF16), vmem((rows, channels), F32),
        dma((9,)), dma(()), pltpu.SemaphoreType.REGULAR, dma((peers,)), dma((peers,)), dma((peers,)), dma((peers,)), dma((seq,)), dma((seq,)),
        dma((3,)), dma((3,)), dma((3, 4)), dma((3, 4)), dma((2, 3)), dma((2, 3)), dma((2, 3)), dma((2, 3)),
        dma((2, 3)), dma((2, 3)), dma((2, 2, 3)), dma((2, 2, 3)), dma((2,)), dma((2,)),
    ]
    own, far = pl.pallas_call(
        kernel,
        out_shape=(jax.ShapeDtypeStruct((rows, channels), F32), jax.ShapeDtypeStruct((2, half, channels), BF16)),
        in_specs=[in_hbm] * 9,
        out_specs=(in_hbm, in_hbm),
        scratch_shapes=scratch,
        compiler_params=pltpu.CompilerParams(collective_id=0, has_side_effects=True, vmem_limit_bytes=62 * 2**20),
        name="hyena",
    )(inner_gate, value_in, outer_gate, filter_taps, out_weight, *(jnp.asarray(c) for c in (f1, f2, g, tw)))
    return own + far.reshape(rows, channels).astype(F32)


def solution(mesh):
    in_specs = (P("seq", "chan"),) * 4 + (P("chan", None),)
    return jax.shard_map(local, mesh=mesh, in_specs=in_specs, out_specs=P("seq", "chan"), check_vma=False)
```

```python
import functools

import jax
import jax.numpy as jnp
import ml_dtypes
import numpy as np
from jax import lax
from jax.experimental import pallas as pl
from jax.experimental.pallas import tpu as pltpu
from jax.sharding import PartitionSpec as P

MESH = pl.DeviceIdType.MESH
NX, NZ, NY = 4, 2, 4
F32, BF16 = jnp.float32, jnp.bfloat16


def split_bf16(values):
    high = values.astype(ml_dtypes.bfloat16)
    low = (values - high.astype(np.float64)).astype(ml_dtypes.bfloat16)
    return np.stack([high, low])


@functools.lru_cache(None)
def transform_constants(blocks, rows, group):
    j, b = np.arange(blocks), np.arange(rows)
    eye = np.eye(group)
    angle = 2 * np.pi * ((4 * j[:, None] + 1) * j[None, :] % (4 * blocks)) / (4 * blocks)
    f1 = np.concatenate([np.kron(np.cos(angle), eye), np.kron(-np.sin(angle), eye)], 0)
    f2 = np.concatenate([np.kron(np.cos(angle).T, eye), np.kron(np.sin(angle).T, eye)], 1) / (blocks * rows)
    turn = 2 * np.pi * ((4 * j[:, None] + 1) * b[None, :]) / (4 * blocks * rows)
    tw = np.stack([np.repeat(np.cos(turn), group, 0), np.repeat(np.sin(turn), group, 0)]).astype(np.float32)
    inner = 2 * np.pi * (b[:, None] * b[None, :] % rows) / rows
    c, s = np.cos(inner), np.sin(inner)
    g = np.block([[c, -s], [s, c]])
    return split_bf16(f1), split_bf16(f2), split_bf16(g), tw


def halves(value):
    high = value.astype(BF16)
    return high, (value - high.astype(F32)).astype(BF16)


def mm(a, b):
    return jnp.dot(a, b, preferred_element_type=F32)


def convolve(hi, lo, taps, f1, f2, g, tw):
    n, rows = hi.shape
    g_hi, g_lo = g[0], g[1]
    cos, sin = tw[0], tw[1]

    def within(re, im):
        high, low = halves(jnp.concatenate([re, im], 1))
        return mm(high, g_hi) + (mm(low, g_hi) + mm(high, g_lo))

    both = jnp.concatenate([hi, taps], 1)
    first = mm(f1[0], both) + mm(f1[1], both)
    sig = first[:, :rows] + mm(f1[0], lo)
    ker = first[:, rows:]

    def turned(re, im):
        return re * cos + im * sin, im * cos - re * sin

    s_re, s_im = turned(sig[:n], sig[n:])
    k_re, k_im = turned(ker[:n], ker[n:])
    spec = within(jnp.concatenate([s_re, k_re], 0), jnp.concatenate([s_im, k_im], 0))
    s_re, s_im = spec[:n, :rows], spec[:n, rows:]
    k_re, k_im = spec[n:, :rows], spec[n:, rows:]
    p_re = s_re * k_re - s_im * k_im
    p_im = -(s_re * k_im + s_im * k_re)
    back = within(p_re, p_im)
    w_re, w_im = turned(back[:, :rows], back[:, rows:])
    high, low = halves(jnp.concatenate([w_re, w_im], 0))
    out = mm(f2[0], jnp.concatenate([high, low], 1))
    return out[:, :rows] + (out[:, rows:] + mm(f2[1], high))


def kernel(
    inner_hbm, value_hbm, outer_hbm, taps_hbm, w_hbm, f1_hbm, f2_hbm, g_hbm, tw_hbm, f1f_hbm, f2f_hbm, twf_hbm, own0_hbm, own1_hbm, far_hbm,
    inner_ref, value_ref, outer_ref, taps_ref, send, send_o, got, got_o, got_f, got_fo, send_g, send_gf, got_g, w, wxa, wxb, f1, f2, g, tw, f1f, f2f, twf, mine, gx, acc0, acc1, s1, r1, s2, r2, zs, own,
    load_sem, own_sem, far_sem, a_ss, a_rs, b_ss, b_rs, p_ss, p_rs, o_ss, o_rs, g_ss, g_rs, h_ss, h_rs, wa_ss, wa_rs, wb_ss, wb_rs, f_ss, f_rs, gx_ss, gx_rs, s1_ss, s1_rs, s2_ss, s2_rs, z_ss, z_rs,
):
    seq = lax.axis_size("seq")
    me, chan = lax.axis_index("seq"), lax.axis_index("chan")
    x, zh, y = lax.div(chan, NZ * NY), lax.rem(lax.div(chan, NY), NZ), lax.rem(chan, NY)
    xs = [x] + [lax.rem(x + d, NX) for d in range(1, NX)]
    ys = [y] + [lax.rem(y + d, NY) for d in range(1, NY)]
    zs_of = [zh, 1 - zh]
    flips = [(1 << b) * (1 - 2 * lax.rem(lax.div(me, 1 << b), 2)) for b in range(seq.bit_length() - 1)]

    def flipped(bits):
        return sum((flip for b, flip in enumerate(flips) if bits >> b & 1), me)
    half, channels = own0_hbm.shape
    rows = 2 * half
    group = channels // seq

    def at(dx, dz, dy):
        return (xs[dx] * NZ + zs_of[dz]) * NY + ys[dy]

    others = [(lax.rem(me + k, seq), chan) for k in range(1, seq)]
    others += [(me, at(d, 0, 0)) for d in range(1, NX)] + [(me, at(0, 0, d)) for d in range(1, NY)]
    barrier = pltpu.get_barrier_semaphore()
    for other in others:
        pl.semaphore_signal(barrier, inc=1, device_id=other, device_id_type=MESH)
    far = (me, at(0, 1, 0))

    @pl.when(zh == 0)
    def _():
        pl.semaphore_signal(barrier, inc=1, device_id=far, device_id_type=MESH)

    pairs = [
        (inner_hbm, inner_ref), (value_hbm, value_ref), (taps_hbm, taps_ref), (outer_hbm, outer_ref),
        (f1_hbm, f1), (f2_hbm, f2), (g_hbm, g), (tw_hbm, tw), (w_hbm, w),
        (f1f_hbm, f1f), (f2f_hbm, f2f), (twf_hbm, twf),
    ]
    loads = [pltpu.make_async_copy(src, dst, load_sem.at[i]) for i, (src, dst) in enumerate(pairs)]
    for load in loads:
        load.start()

    loads[0].wait()
    loads[1].wait()
    signal = (inner_ref[...].astype(F32) * value_ref[...].astype(F32)).T
    hi, lo = halves(signal)
    send[:, 0:group] = hi.reshape(seq, group, rows)
    send[:, group : 2 * group] = lo.reshape(seq, group, rows)
    loads[2].wait()
    send[:, 2 * group : 3 * group] = taps_ref[...].astype(F32).T.astype(BF16).reshape(seq, group, rows)
    loads[3].wait()
    send_o[...] = outer_ref[...].astype(F32).T.astype(BF16).reshape(seq, group, rows)
    pl.semaphore_wait(barrier, len(others) + zh)

    @pl.when(zh == 1)
    def _():
        pl.semaphore_signal(far_sem, inc=1, device_id=far, device_id_type=MESH)

    def remote(src, dst, ss, rs, dx=0, dz=0, dy=0, to=None):
        copy = pltpu.make_async_remote_copy(
            src_ref=src, dst_ref=dst, send_sem=ss, recv_sem=rs,
            device_id=(me, at(dx, dz, dy)) if to is None else to, device_id_type=MESH,
        )
        copy.start()
        return copy

    mid = seq // 2
    first, second_half = me < mid, me >= mid

    def to_first(k, gates=False):
        to = flipped(k)
        src, dst, ss, rs = (send_o, got_fo, p_ss, p_rs) if gates else (send, got_f, b_ss, b_rs)
        return pltpu.make_async_remote_copy(
            src_ref=src.at[pl.ds(2 * to, 2)], dst_ref=dst.at[me], send_sem=ss.at[k - 1], recv_sem=rs.at[k - 1],
            device_id=(to, chan), device_id_type=MESH,
        )

    @pl.when(first)
    def _():
        for k in reversed(range(1, mid)):
            to_first(k).start()
        got_f[me] = send[pl.ds(2 * me, 2)]
        got_fo[me] = send_o[pl.ds(2 * me, 2)]

    def across(ks):
        copies = []
        for k in ks:
            to = flipped(k)
            copies.append(remote(send.at[to], got.at[me], a_ss.at[k - 1], a_rs.at[k - 1], to=(to, chan)))
        return copies

    out_a = across(reversed(range(mid, seq)))

    @pl.when(first)
    def _():
        for k in reversed(range(1, mid)):
            to_first(k, True).start()

    out_a += across(reversed(range(1, mid)))
    got[me] = send[me]

    def outer_to(k):
        to = flipped(k)
        return pltpu.make_async_remote_copy(
            src_ref=send_o.at[to], dst_ref=got_o.at[me - mid], send_sem=o_ss.at[k - 1], recv_sem=o_rs.at[me - mid],
            device_id=(to, chan), device_id_type=MESH,
        )

    def outer_from(i):
        return pltpu.make_async_remote_copy(
            src_ref=send_o.at[i], dst_ref=got_o.at[i], send_sem=o_ss.at[i], recv_sem=o_rs.at[i],
            device_id=(mid + i, chan), device_id_type=MESH,
        )

    @pl.when(second_half)
    def _():
        for k in reversed(range(1, seq)):
            outer_to(k).start()
        got_o[me - mid] = send_o[me]

    order, width = [2, 1, 3, 0], channels
    core = lax.rem(me, 2)
    sibling = (me + 1 - 2 * core, chan)
    part = pl.ds(pl.multiple_of(core * (channels // 2), channels // 2), channels // 2)
    weights, onward = {}, []

    def pass_on(d):
        weights[0, d].wait_recv()
        onward.append(remote(wxa.at[d - 1, part], wxa.at[d - 1, part], f_ss.at[0, d - 1], f_rs.at[0, d - 1], to=sibling))
        for i in range(NX):
            weights[1, d, i].wait_recv()
        onward.append(remote(wxb.at[d - 1, :, part], wxb.at[d - 1, :, part], f_ss.at[1, d - 1], f_rs.at[1, d - 1], to=sibling))

    loads[8].wait()
    for d in (1, 3, 2):
        column = pl.multiple_of((xs[d] * NZ + 1 - zh) * NY * width, NY * width)
        weights[0, d] = remote(
            w.at[part, pl.ds(column, NY * width)], wxa.at[d - 1, part], wa_ss.at[d - 1], wa_rs.at[d - 1], dx=d
        )
        for i in range(NX):
            column = pl.multiple_of(((i * NZ + 1 - zh) * NY + ys[d]) * width, width)
            weights[1, d, i] = remote(
                w.at[part, pl.ds(column, width)], wxb.at[d - 1, i, part], wb_ss.at[d - 1, i], wb_rs.at[d - 1, i], dy=d
            )
    for load in loads[4:8] + loads[9:]:
        load.wait()
    n = seq * group

    def back_first(to, source):
        return pltpu.make_async_remote_copy(
            src_ref=send_gf.at[to], dst_ref=got_g.at[pl.ds(2 * source, 2)], send_sem=h_ss.at[to], recv_sem=h_rs.at[source],
            device_id=(to, chan), device_id_type=MESH,
        )

    def back_second(i, source):
        return pltpu.make_async_remote_copy(
            src_ref=send_g.at[i], dst_ref=got_g.at[source], send_sem=g_ss.at[i], recv_sem=g_rs.at[source],
            device_id=(mid + i, chan), device_id_type=MESH,
        )

    @pl.when(first)
    def _():
        for k in range(1, mid):
            to_first(k).wait_recv()
        conv = convolve(
            got_f[:, :, 0:group].reshape(n, rows), got_f[:, :, group : 2 * group].reshape(n, rows),
            got_f[:, :, 2 * group : 3 * group].reshape(n, rows), f1f, f2f, g, twf,
        )
        for k in range(1, mid):
            to_first(k, True).wait_recv()
        gated = (got_fo[...].reshape(n, rows).astype(F32) * conv).astype(BF16)
        send_gf[...] = gated.reshape(mid, 2, group, rows)
        for i in range(mid - 1):
            back_first(i + (i >= me).astype(jnp.int32), me).start()
        got_g[pl.ds(2 * me, 2)] = send_gf[me]

    pass_on(1)
    pass_on(3)
    for copy in out_a:
        copy.wait_recv()
    conv = convolve(
        got[:, 0:group].reshape(n, rows), got[:, group : 2 * group].reshape(n, rows),
        got[:, 2 * group : 3 * group].reshape(n, rows), f1, f2, g, tw,
    )
    for i in range(mid):

        @pl.when(me != mid + i)
        def _():
            outer_from(i).wait_recv()

    gated = (got_o[...].reshape(n // 2, rows).astype(F32) * conv).astype(BF16)
    send_g[...] = gated.reshape(mid, group, rows)
    for i in range(mid):

        @pl.when(me != mid + i)
        def _():
            back_second(i, me).start()

    @pl.when(second_half)
    def _():
        got_g[me] = send_g[me - mid]

    pass_on(2)

    @pl.when(first)
    def _():
        for k in range(1, mid):
            back_first(me, flipped(k)).wait_recv()

    @pl.when(second_half)
    def _():
        for k in range(1, seq):
            back_second(me - mid, flipped(k)).wait_recv()

    mine[...] = got_g[...].reshape(n, rows).astype(F32).T.astype(BF16)

    gather, stage1, stage2, last = {}, {}, {}, []
    for d in order[:3]:
        for h in range(2):
            gather[h, d] = remote(
                mine.at[pl.ds(h * half, half)], gx.at[h, d - 1], gx_ss.at[h, d - 1], gx_rs.at[h, d - 1],
                d * (1 - h), 0, d * h,
            )
    for i in range(4):
        for h in range(2):
            block = (x * NZ + 1 - zh) * NY + i if h == 0 else (i * NZ + 1 - zh) * NY + y
            column = pl.multiple_of(block * width, width)
            acc0[h, i] = mm(mine[h * half : (h + 1) * half], w[:, pl.ds(column, width)])
    for dx in order:
        for dy in order:
            column = pl.multiple_of(at(dx, 0, dy) * width, width)
            block = mm(mine[...], w[:, pl.ds(column, width)])
            if dx == 0:
                acc1[0, dy] = block[:half]
            else:
                s1[0, dx - 1, :, dy * width : (dy + 1) * width] = block[:half].astype(BF16)
            if dy == 0:
                acc1[1, dx] = block[half:]
            else:
                s1[1, dy - 1, :, dx * width : (dx + 1) * width] = block[half:].astype(BF16)
    for copy in onward:
        copy.wait_recv()
    for d in (1, 3, 2):
        for h in range(2):
            gather[h, d].wait_recv()
            for i in range(4):
                block = wxa[d - 1, :, i * width : (i + 1) * width] if h == 0 else wxb[d - 1, i]
                acc0[h, i] += mm(gx[h, d - 1], block)

    def second(wave, h, d, total):
        s2[wave, h, d - 1] = total.astype(BF16)
        stage2[wave, h, d] = remote(
            s2.at[wave, h, d - 1], r2.at[wave, h, d - 1], s2_ss.at[wave, h, d - 1], s2_rs.at[wave, h, d - 1],
            d * h, 0, d * (1 - h),
        )

    def finished(wave, h, total):
        for d in (1, 3, 2):
            stage2[wave, h, d].wait_recv()
            total = total + r2[wave, h, d - 1].astype(F32)
        return total

    for d in order[:3]:
        for h in range(2):
            second(0, h, d, acc0[h, ys[d] if h == 0 else xs[d]])
    for d in order[:3]:
        for h in range(2):
            stage1[h, d] = remote(
                s1.at[h, d - 1], r1.at[h, d - 1], s1_ss.at[h, d - 1], s1_rs.at[h, d - 1], d * (1 - h), 0, d * h
            )
    for h in range(2):
        total = finished(0, h, acc0[h, y if h == 0 else x])
        if h == 0:

            @pl.when(zh == 0)
            def _():
                pl.semaphore_wait(far_sem, 1)

        zs[h] = total.astype(BF16)
        last.append(remote(zs.at[h], far_hbm.at[h], z_ss.at[h], z_rs.at[h], 0, 1, 0))
    for h in range(2):
        for d in (1, 3, 2):
            stage1[h, d].wait_recv()
        for d in order:
            total = acc1[h, d]
            for e in range(3):
                total = total + r1[h, e, :, d * width : (d + 1) * width].astype(F32)
            if d:
                second(1, h, d, total)
            else:
                acc1[h, 0] = total
    stores = []
    for h in range(2):
        own[h] = finished(1, h, acc1[h, 0])
        stores.append(pltpu.make_async_copy(own.at[h], (own0_hbm, own1_hbm)[h], own_sem.at[h]))
        stores[h].start()
    for copy in last:
        copy.wait_recv()
    for store in stores:
        store.wait()
    groups = (weights, gather, stage1, stage2)
    @pl.when(first)
    def _():
        for k in range(1, mid):
            to_first(k).wait_send()
            to_first(k, True).wait_send()
        for i in range(mid - 1):
            back_first(i + (i >= me).astype(jnp.int32), me).wait_send()

    @pl.when(second_half)
    def _():
        for k in range(1, seq):
            outer_to(k).wait_send()

    for i in range(mid):

        @pl.when(me != mid + i)
        def _():
            back_second(i, me).wait_send()

    for copy in out_a + onward + last + [copy for g in groups for copy in g.values()]:
        copy.wait_send()


def local(inner_gate, value_in, outer_gate, filter_taps, out_weight):
    rows, channels = inner_gate.shape
    seq = lax.axis_size("seq")
    group, half = channels // seq, rows // 2
    f1, f2, g, tw = transform_constants(seq, rows, group)
    f2 = f2[:, f2.shape[1] // 2 :]
    f1f, f2f, _, twf = transform_constants(seq // 2, rows, 2 * group)
    vmem, dma = pltpu.VMEM, pltpu.SemaphoreType.DMA
    in_hbm, in_any = pl.BlockSpec(memory_space=pltpu.HBM), pl.BlockSpec(memory_space=pl.ANY)
    peers, mid = seq - 1, seq // 2
    scratch = [
        *[vmem((rows, channels), BF16)] * 4,
        vmem((seq, 3 * group, rows), BF16), vmem((seq, group, rows), BF16),
        vmem((seq, 3 * group, rows), BF16), vmem((mid, group, rows), BF16),
        vmem((mid, 2, 3 * group, rows), BF16), vmem((mid, 2, group, rows), BF16),
        vmem((mid, group, rows), BF16), vmem((mid, 2, group, rows), BF16), vmem((seq, group, rows), BF16),
        vmem(out_weight.shape, BF16), vmem((3, channels, NY * channels), BF16), vmem((3, NX, channels, channels), BF16),
        vmem(f1.shape, BF16), vmem(f2.shape, BF16), vmem(g.shape, BF16), vmem(tw.shape, F32),
        vmem(f1f.shape, BF16), vmem(f2f.shape, BF16), vmem(twf.shape, F32),
        vmem((rows, channels), BF16), vmem((2, 3, half, channels), BF16),
        vmem((2, 4, half, channels), F32), vmem((2, 4, half, channels), F32),
        vmem((2, 3, half, 4 * channels), BF16), vmem((2, 3, half, 4 * channels), BF16),
        vmem((2, 2, 3, half, channels), BF16), vmem((2, 2, 3, half, channels), BF16),
        vmem((2, half, channels), BF16), vmem((2, half, channels), F32),
        dma((12,)), dma((2,)), pltpu.SemaphoreType.REGULAR, dma((peers,)), dma((peers,)), *[dma((mid - 1,))] * 4, dma((peers,)), dma((mid,)),
        dma((mid,)), dma((seq,)), dma((mid,)), dma((mid,)),
        dma((3,)), dma((3,)), dma((3, 4)), dma((3, 4)), dma((2, 3)), dma((2, 3)), dma((2, 3)), dma((2, 3)),
        dma((2, 3)), dma((2, 3)), dma((2, 2, 3)), dma((2, 2, 3)), dma((2,)), dma((2,)),
    ]
    *own, far = pl.pallas_call(
        kernel,
        out_shape=(*[jax.ShapeDtypeStruct((half, channels), F32)] * 2, jax.ShapeDtypeStruct((2, half, channels), BF16)),
        in_specs=[in_hbm] * 12,
        out_specs=(in_any,) * 3,
        scratch_shapes=scratch,
        compiler_params=pltpu.CompilerParams(collective_id=0, has_side_effects=True, vmem_limit_bytes=5372 * 2**20 // 100),
        name="hyena",
    )(inner_gate, value_in, outer_gate, filter_taps, out_weight, *(jnp.asarray(c) for c in (f1, f2, g, tw, f1f, f2f, twf)))
    return jnp.concatenate([part + far[h].astype(F32) for h, part in enumerate(own)], 0)


def solution(mesh):
    in_specs = (P("seq", "chan"),) * 4 + (P("chan", None),)
    return jax.shard_map(local, mesh=mesh, in_specs=in_specs, out_specs=P("seq", "chan"), check_vma=False)
```

```python
import functools

import jax
import jax.numpy as jnp
import ml_dtypes
import numpy as np
from jax import lax
from jax.experimental import pallas as pl
from jax.experimental.pallas import tpu as pltpu
from jax.sharding import PartitionSpec as P

MESH = pl.DeviceIdType.MESH
NX, NZ, NY = 4, 2, 4
F32, BF16 = jnp.float32, jnp.bfloat16


def split_bf16(values):
    high = values.astype(ml_dtypes.bfloat16)
    low = (values - high.astype(np.float64)).astype(ml_dtypes.bfloat16)
    return np.stack([high, low])


@functools.lru_cache(None)
def transform_constants(blocks, rows, group):
    j, b = np.arange(blocks), np.arange(rows)
    eye = np.eye(group)
    angle = 2 * np.pi * ((4 * j[:, None] + 1) * j[None, :] % (4 * blocks)) / (4 * blocks)
    f1 = np.concatenate([np.kron(np.cos(angle), eye), np.kron(-np.sin(angle), eye)], 0)
    f2 = np.concatenate([np.kron(np.cos(angle).T, eye), np.kron(np.sin(angle).T, eye)], 1) / (blocks * rows)
    turn = 2 * np.pi * ((4 * j[:, None] + 1) * b[None, :]) / (4 * blocks * rows)
    tw = np.stack([np.repeat(np.cos(turn), group, 0), np.repeat(np.sin(turn), group, 0)]).astype(np.float32)
    inner = 2 * np.pi * (b[:, None] * b[None, :] % rows) / rows
    c, s = np.cos(inner), np.sin(inner)
    g = np.block([[c, -s], [s, c]])
    return split_bf16(f1), split_bf16(f2), split_bf16(g), tw


def halves(value):
    high = value.astype(BF16)
    return high, (value - high.astype(F32)).astype(BF16)


def mm(a, b):
    return jnp.dot(a, b, preferred_element_type=F32)


def convolve(hi, lo, taps, f1, f2, g, tw):
    n, rows = hi.shape
    g_hi, g_lo = g[0], g[1]
    cos, sin = tw[0], tw[1]

    def within(re, im):
        high, low = halves(jnp.concatenate([re, im], 1))
        return mm(high, g_hi) + (mm(low, g_hi) + mm(high, g_lo))

    both = jnp.concatenate([hi, taps], 1)
    first = mm(f1[0], both) + mm(f1[1], both)
    sig = first[:, :rows] + mm(f1[0], lo)
    ker = first[:, rows:]

    def turned(re, im):
        return re * cos + im * sin, im * cos - re * sin

    s_re, s_im = turned(sig[:n], sig[n:])
    k_re, k_im = turned(ker[:n], ker[n:])
    spec = within(jnp.concatenate([s_re, k_re], 0), jnp.concatenate([s_im, k_im], 0))
    s_re, s_im = spec[:n, :rows], spec[:n, rows:]
    k_re, k_im = spec[n:, :rows], spec[n:, rows:]
    p_re = s_re * k_re - s_im * k_im
    p_im = -(s_re * k_im + s_im * k_re)
    back = within(p_re, p_im)
    w_re, w_im = turned(back[:, :rows], back[:, rows:])
    high, low = halves(jnp.concatenate([w_re, w_im], 0))
    out = mm(f2[0], jnp.concatenate([high, low], 1))
    return out[:, :rows] + (out[:, rows:] + mm(f2[1], high))


def kernel(
    inner_hbm, value_hbm, outer_hbm, taps_hbm, w_hbm, f1_hbm, f2_hbm, g_hbm, tw_hbm, f1f_hbm, f2f_hbm, twf_hbm, own0_hbm, own1_hbm, far_hbm,
    inner_ref, value_ref, outer_ref, taps_ref, send, send_o, got, got_o, got_f, got_fo, send_g, send_gf, got_g, w, wxa, wxb, f1, f2, g, tw, f1f, f2f, twf, mine, gx, acc0, acc1, s1, r1, s2, r2, zs, own,
    load_sem, own_sem, far_sem, a_ss, a_rs, b_ss, b_rs, p_ss, p_rs, o_ss, o_rs, g_ss, g_rs, h_ss, h_rs, wa_ss, wa_rs, wb_ss, wb_rs, f_ss, f_rs, gx_ss, gx_rs, s1_ss, s1_rs, s2_ss, s2_rs, z_ss, z_rs,
):
    seq = lax.axis_size("seq")
    me, chan = lax.axis_index("seq"), lax.axis_index("chan")
    x, zh, y = lax.div(chan, NZ * NY), lax.rem(lax.div(chan, NY), NZ), lax.rem(chan, NY)
    xs = [x] + [lax.rem(x + d, NX) for d in range(1, NX)]
    ys = [y] + [lax.rem(y + d, NY) for d in range(1, NY)]
    zs_of = [zh, 1 - zh]
    flips = [(1 << b) * (1 - 2 * lax.rem(lax.div(me, 1 << b), 2)) for b in range(seq.bit_length() - 1)]

    def flipped(bits):
        return sum((flip for b, flip in enumerate(flips) if bits >> b & 1), me)
    half, channels = own0_hbm.shape
    rows = 2 * half
    group = channels // seq

    def at(dx, dz, dy):
        return (xs[dx] * NZ + zs_of[dz]) * NY + ys[dy]

    others = [(lax.rem(me + k, seq), chan) for k in range(1, seq)]
    others += [(me, at(d, 0, 0)) for d in range(1, NX)] + [(me, at(0, 0, d)) for d in range(1, NY)]
    barrier = pltpu.get_barrier_semaphore()
    for other in others:
        pl.semaphore_signal(barrier, inc=1, device_id=other, device_id_type=MESH)
    far = (me, at(0, 1, 0))

    @pl.when(zh == 0)
    def _():
        pl.semaphore_signal(barrier, inc=1, device_id=far, device_id_type=MESH)

    pairs = [
        (inner_hbm, inner_ref), (value_hbm, value_ref), (taps_hbm, taps_ref), (outer_hbm, outer_ref),
        (f1_hbm, f1), (f2_hbm, f2), (g_hbm, g), (tw_hbm, tw), (w_hbm, w),
        (f1f_hbm, f1f), (f2f_hbm, f2f), (twf_hbm, twf),
    ]
    loads = [pltpu.make_async_copy(src, dst, load_sem.at[i]) for i, (src, dst) in enumerate(pairs)]
    for load in loads:
        load.start()

    loads[0].wait()
    loads[1].wait()
    signal = (inner_ref[...].astype(F32) * value_ref[...].astype(F32)).T
    hi, lo = halves(signal)
    send[:, 0:group] = hi.reshape(seq, group, rows)
    send[:, group : 2 * group] = lo.reshape(seq, group, rows)
    loads[2].wait()
    send[:, 2 * group : 3 * group] = taps_ref[...].astype(F32).T.astype(BF16).reshape(seq, group, rows)
    loads[3].wait()
    send_o[...] = outer_ref[...].astype(F32).T.astype(BF16).reshape(seq, group, rows)
    pl.semaphore_wait(barrier, len(others) + zh)

    @pl.when(zh == 1)
    def _():
        pl.semaphore_signal(far_sem, inc=1, device_id=far, device_id_type=MESH)

    def remote(src, dst, ss, rs, dx=0, dz=0, dy=0, to=None):
        copy = pltpu.make_async_remote_copy(
            src_ref=src, dst_ref=dst, send_sem=ss, recv_sem=rs,
            device_id=(me, at(dx, dz, dy)) if to is None else to, device_id_type=MESH,
        )
        copy.start()
        return copy

    mid = seq // 2
    first, second_half = me < mid, me >= mid

    def block_of(device):
        return 2 * lax.rem(device, mid) + lax.div(device, mid)


    def to_first(k, gates=False):
        to = flipped(k)
        src, dst, ss, rs = (send_o, got_fo, p_ss, p_rs) if gates else (send, got_f, b_ss, b_rs)
        return pltpu.make_async_remote_copy(
            src_ref=src.at[pl.ds(2 * to, 2)], dst_ref=dst.at[me], send_sem=ss.at[k - 1], recv_sem=rs.at[k - 1],
            device_id=(to, chan), device_id_type=MESH,
        )

    @pl.when(first)
    def _():
        for k in reversed(range(1, mid)):
            to_first(k).start()
        got_f[me] = send[pl.ds(2 * me, 2)]
        got_fo[me] = send_o[pl.ds(2 * me, 2)]

    def full_to(k):
        to = flipped(k)
        return pltpu.make_async_remote_copy(
            src_ref=send.at[block_of(to)], dst_ref=got.at[me], send_sem=a_ss.at[k - 1], recv_sem=a_rs.at[k - 1],
            device_id=(to, chan), device_id_type=MESH,
        )

    def outer_to(k):
        to = flipped(k)
        return pltpu.make_async_remote_copy(
            src_ref=send_o.at[block_of(to)], dst_ref=got_o.at[me - mid], send_sem=o_ss.at[k - 1], recv_sem=o_rs.at[me - mid],
            device_id=(to, chan), device_id_type=MESH,
        )

    across, near = list(reversed(range(mid, seq))), list(reversed(range(1, mid)))
    for k in across:
        full_to(k).start()

    @pl.when(first)
    def _():
        for k in near:
            to_first(k, True).start()

    @pl.when(second_half)
    def _():
        for k in near:
            full_to(k).start()
        for k in across + near:
            outer_to(k).start()
        got[me] = send[block_of(me)]
        got_o[me - mid] = send_o[block_of(me)]

    def outer_from(i):
        return pltpu.make_async_remote_copy(
            src_ref=send_o.at[i], dst_ref=got_o.at[i], send_sem=o_ss.at[i], recv_sem=o_rs.at[i],
            device_id=(mid + i, chan), device_id_type=MESH,
        )

    order, width = [2, 1, 3, 0], channels
    core = lax.rem(me, 2)
    sibling = (me + 1 - 2 * core, chan)
    part = pl.ds(pl.multiple_of(core * (channels // 2), channels // 2), channels // 2)
    weights, onward = {}, []

    def pass_on(d):
        weights[0, d].wait_recv()
        onward.append(remote(wxa.at[d - 1, part], wxa.at[d - 1, part], f_ss.at[0, d - 1], f_rs.at[0, d - 1], to=sibling))
        for i in range(NX):
            weights[1, d, i].wait_recv()
        onward.append(remote(wxb.at[d - 1, :, part], wxb.at[d - 1, :, part], f_ss.at[1, d - 1], f_rs.at[1, d - 1], to=sibling))

    loads[8].wait()
    for d in (1, 3, 2):
        column = pl.multiple_of((xs[d] * NZ + 1 - zh) * NY * width, NY * width)
        weights[0, d] = remote(
            w.at[part, pl.ds(column, NY * width)], wxa.at[d - 1, part], wa_ss.at[d - 1], wa_rs.at[d - 1], dx=d
        )
        for i in range(NX):
            column = pl.multiple_of(((i * NZ + 1 - zh) * NY + ys[d]) * width, width)
            weights[1, d, i] = remote(
                w.at[part, pl.ds(column, width)], wxb.at[d - 1, i, part], wb_ss.at[d - 1, i], wb_rs.at[d - 1, i], dy=d
            )
    for load in loads[4:8] + loads[9:]:
        load.wait()
    n = seq * group

    def back_first(to, source):
        return pltpu.make_async_remote_copy(
            src_ref=send_gf.at[to], dst_ref=got_g.at[pl.ds(2 * source, 2)], send_sem=h_ss.at[to], recv_sem=h_rs.at[source],
            device_id=(to, chan), device_id_type=MESH,
        )

    def back_second(i, source):
        return pltpu.make_async_remote_copy(
            src_ref=send_g.at[i], dst_ref=got_g.at[block_of(source)], send_sem=g_ss.at[i], recv_sem=g_rs.at[source],
            device_id=(mid + i, chan), device_id_type=MESH,
        )

    @pl.when(first)
    def _():
        for k in range(1, mid):
            to_first(k).wait_recv()
        conv = convolve(
            got_f[:, :, 0:group].reshape(n, rows), got_f[:, :, group : 2 * group].reshape(n, rows),
            got_f[:, :, 2 * group : 3 * group].reshape(n, rows), f1f, f2f, g, twf,
        )
        for k in range(1, mid):
            to_first(k, True).wait_recv()
        gated = (got_fo[...].reshape(n, rows).astype(F32) * conv).astype(BF16)
        send_gf[...] = gated.reshape(mid, 2, group, rows)
        for i in range(mid - 1):
            back_first(i + (i >= me).astype(jnp.int32), me).start()
        got[:mid] = got_f[:, 0]
        got_g[pl.ds(2 * me, 2)] = send_gf[me]

    pass_on(1)
    pass_on(3)
    for k in across:
        full_to(k).wait_recv()

    @pl.when(second_half)
    def _():
        for k in near:
            full_to(k).wait_recv()

    conv = convolve(
        got[:, 0:group].reshape(n, rows), got[:, group : 2 * group].reshape(n, rows),
        got[:, 2 * group : 3 * group].reshape(n, rows), f1, f2, g, tw,
    )
    for i in range(mid):

        @pl.when(me != mid + i)
        def _():
            outer_from(i).wait_recv()

    gated = (got_o[...].reshape(n // 2, rows).astype(F32) * conv).astype(BF16)
    send_g[...] = gated.reshape(mid, group, rows)
    for i in range(mid):

        @pl.when(me != mid + i)
        def _():
            back_second(i, me).start()

    @pl.when(second_half)
    def _():
        got_g[block_of(me)] = send_g[me - mid]

    pass_on(2)

    @pl.when(first)
    def _():
        for k in range(1, mid):
            back_first(me, flipped(k)).wait_recv()

    @pl.when(second_half)
    def _():
        for k in range(1, seq):
            back_second(me - mid, flipped(k)).wait_recv()

    mine[...] = got_g[...].reshape(n, rows).astype(F32).T.astype(BF16)

    gather, stage1, stage2, last = {}, {}, {}, []
    for d in order[:3]:
        for h in range(2):
            gather[h, d] = remote(
                mine.at[pl.ds(h * half, half)], gx.at[h, d - 1], gx_ss.at[h, d - 1], gx_rs.at[h, d - 1],
                d * (1 - h), 0, d * h,
            )
    for i in range(4):
        for h in range(2):
            block = (x * NZ + 1 - zh) * NY + i if h == 0 else (i * NZ + 1 - zh) * NY + y
            column = pl.multiple_of(block * width, width)
            acc0[h, i] = mm(mine[h * half : (h + 1) * half], w[:, pl.ds(column, width)])
    for dx in order:
        for dy in order:
            column = pl.multiple_of(at(dx, 0, dy) * width, width)
            block = mm(mine[...], w[:, pl.ds(column, width)])
            if dx == 0:
                acc1[0, dy] = block[:half]
            else:
                s1[0, dx - 1, :, dy * width : (dy + 1) * width] = block[:half].astype(BF16)
            if dy == 0:
                acc1[1, dx] = block[half:]
            else:
                s1[1, dy - 1, :, dx * width : (dx + 1) * width] = block[half:].astype(BF16)
    for d in order[:1]:
        for h in range(2):
            stage1[h, d] = remote(
                s1.at[h, d - 1], r1.at[h, d - 1], s1_ss.at[h, d - 1], s1_rs.at[h, d - 1], d * (1 - h), 0, d * h
            )
    for copy in onward:
        copy.wait_recv()
    for d in (1, 3, 2):
        for h in range(2):
            gather[h, d].wait_recv()
            for i in range(4):
                block = wxa[d - 1, :, i * width : (i + 1) * width] if h == 0 else wxb[d - 1, i]
                acc0[h, i] += mm(gx[h, d - 1], block)

    def second(wave, h, d, total):
        s2[wave, h, d - 1] = total.astype(BF16)
        stage2[wave, h, d] = remote(
            s2.at[wave, h, d - 1], r2.at[wave, h, d - 1], s2_ss.at[wave, h, d - 1], s2_rs.at[wave, h, d - 1],
            d * h, 0, d * (1 - h),
        )

    def finished(wave, h, total):
        for d in (1, 3, 2):
            stage2[wave, h, d].wait_recv()
            total = total + r2[wave, h, d - 1].astype(F32)
        return total

    for d in order[:3]:
        for h in range(2):
            second(0, h, d, acc0[h, ys[d] if h == 0 else xs[d]])
    for d in order[1:3]:
        for h in range(2):
            stage1[h, d] = remote(
                s1.at[h, d - 1], r1.at[h, d - 1], s1_ss.at[h, d - 1], s1_rs.at[h, d - 1], d * (1 - h), 0, d * h
            )
    for h in range(2):
        total = finished(0, h, acc0[h, y if h == 0 else x])
        if h == 0:

            @pl.when(zh == 0)
            def _():
                pl.semaphore_wait(far_sem, 1)

        zs[h] = total.astype(BF16)
        last.append(remote(zs.at[h], far_hbm.at[h], z_ss.at[h], z_rs.at[h], 0, 1, 0))
    for h in range(2):
        for d in (1, 3, 2):
            stage1[h, d].wait_recv()
        for d in order:
            total = acc1[h, d]
            for e in range(3):
                total = total + r1[h, e, :, d * width : (d + 1) * width].astype(F32)
            if d:
                second(1, h, d, total)
            else:
                acc1[h, 0] = total
    stores = []
    for h in range(2):
        own[h] = finished(1, h, acc1[h, 0])
        stores.append(pltpu.make_async_copy(own.at[h], (own0_hbm, own1_hbm)[h], own_sem.at[h]))
        stores[h].start()
    for copy in last:
        copy.wait_recv()
    for store in stores:
        store.wait()
    groups = (weights, gather, stage1, stage2)
    @pl.when(first)
    def _():
        for k in range(1, mid):
            to_first(k).wait_send()
            to_first(k, True).wait_send()
        for i in range(mid - 1):
            back_first(i + (i >= me).astype(jnp.int32), me).wait_send()

    @pl.when(second_half)
    def _():
        for k in across + near:
            outer_to(k).wait_send()
        for k in near:
            full_to(k).wait_send()

    for k in across:
        full_to(k).wait_send()

    for i in range(mid):

        @pl.when(me != mid + i)
        def _():
            back_second(i, me).wait_send()

    for copy in onward + last + [copy for g in groups for copy in g.values()]:
        copy.wait_send()


def local(inner_gate, value_in, outer_gate, filter_taps, out_weight):
    rows, channels = inner_gate.shape
    seq = lax.axis_size("seq")
    group, half = channels // seq, rows // 2
    f1, f2, g, tw = transform_constants(seq, rows, group)
    f2 = f2[:, f2.shape[1] // 2 :]
    f1f, f2f, _, twf = transform_constants(seq // 2, rows, 2 * group)
    vmem, dma = pltpu.VMEM, pltpu.SemaphoreType.DMA
    in_hbm, in_any = pl.BlockSpec(memory_space=pltpu.HBM), pl.BlockSpec(memory_space=pl.ANY)
    peers, mid = seq - 1, seq // 2
    scratch = [
        *[vmem((rows, channels), BF16)] * 4,
        vmem((seq, 3 * group, rows), BF16), vmem((seq, group, rows), BF16),
        vmem((seq, 3 * group, rows), BF16), vmem((mid, group, rows), BF16),
        vmem((mid, 2, 3 * group, rows), BF16), vmem((mid, 2, group, rows), BF16),
        vmem((mid, group, rows), BF16), vmem((mid, 2, group, rows), BF16), vmem((seq, group, rows), BF16),
        vmem(out_weight.shape, BF16), vmem((3, channels, NY * channels), BF16), vmem((3, NX, channels, channels), BF16),
        vmem(f1.shape, BF16), vmem(f2.shape, BF16), vmem(g.shape, BF16), vmem(tw.shape, F32),
        vmem(f1f.shape, BF16), vmem(f2f.shape, BF16), vmem(twf.shape, F32),
        vmem((rows, channels), BF16), vmem((2, 3, half, channels), BF16),
        vmem((2, 4, half, channels), F32), vmem((2, 4, half, channels), F32),
        vmem((2, 3, half, 4 * channels), BF16), vmem((2, 3, half, 4 * channels), BF16),
        vmem((2, 2, 3, half, channels), BF16), vmem((2, 2, 3, half, channels), BF16),
        vmem((2, half, channels), BF16), vmem((2, half, channels), F32),
        dma((12,)), dma((2,)), pltpu.SemaphoreType.REGULAR, dma((peers,)), dma((peers,)), *[dma((mid - 1,))] * 4, dma((peers,)), dma((mid,)),
        dma((mid,)), dma((seq,)), dma((mid,)), dma((mid,)),
        dma((3,)), dma((3,)), dma((3, 4)), dma((3, 4)), dma((2, 3)), dma((2, 3)), dma((2, 3)), dma((2, 3)),
        dma((2, 3)), dma((2, 3)), dma((2, 2, 3)), dma((2, 2, 3)), dma((2,)), dma((2,)),
    ]
    *own, far = pl.pallas_call(
        kernel,
        out_shape=(*[jax.ShapeDtypeStruct((half, channels), F32)] * 2, jax.ShapeDtypeStruct((2, half, channels), BF16)),
        in_specs=[in_hbm] * 12,
        out_specs=(in_any,) * 3,
        scratch_shapes=scratch,
        compiler_params=pltpu.CompilerParams(collective_id=0, has_side_effects=True, vmem_limit_bytes=5372 * 2**20 // 100),
        name="hyena",
    )(inner_gate, value_in, outer_gate, filter_taps, out_weight, *(jnp.asarray(c) for c in (f1, f2, g, tw, f1f, f2f, twf)))
    return jnp.concatenate([part + far[h].astype(F32) for h, part in enumerate(own)], 0)


def solution(mesh):
    in_specs = (P("seq", "chan"),) * 4 + (P("chan", None),)
    return jax.shard_map(local, mesh=mesh, in_specs=in_specs, out_specs=P("seq", "chan"), check_vma=False)
```

```python
import functools

import jax
import jax.numpy as jnp
import ml_dtypes
import numpy as np
from jax import lax
from jax.experimental import pallas as pl
from jax.experimental.pallas import tpu as pltpu
from jax.sharding import PartitionSpec as P

MESH = pl.DeviceIdType.MESH
NX, NZ, NY = 4, 2, 4
F32, BF16 = jnp.float32, jnp.bfloat16


def split_bf16(values):
    high = values.astype(ml_dtypes.bfloat16)
    low = (values - high.astype(np.float64)).astype(ml_dtypes.bfloat16)
    return np.stack([high, low])


@functools.lru_cache(None)
def transform_constants(blocks, rows, group):
    j, b = np.arange(blocks), np.arange(rows)
    eye = np.eye(group)
    angle = 2 * np.pi * ((4 * j[:, None] + 1) * j[None, :] % (4 * blocks)) / (4 * blocks)
    f1 = np.concatenate([np.kron(np.cos(angle), eye), np.kron(-np.sin(angle), eye)], 0)
    f2 = np.concatenate([np.kron(np.cos(angle).T, eye), np.kron(np.sin(angle).T, eye)], 1) / (blocks * rows)
    turn = 2 * np.pi * ((4 * j[:, None] + 1) * b[None, :]) / (4 * blocks * rows)
    tw = np.stack([np.repeat(np.cos(turn), group, 0), np.repeat(np.sin(turn), group, 0)]).astype(np.float32)
    inner = 2 * np.pi * (b[:, None] * b[None, :] % rows) / rows
    c, s = np.cos(inner), np.sin(inner)
    g = np.block([[c, -s], [s, c]])
    return split_bf16(f1), split_bf16(f2), split_bf16(g), tw


def halves(value):
    high = value.astype(BF16)
    return high, (value - high.astype(F32)).astype(BF16)


def mm(a, b):
    return jnp.dot(a, b, preferred_element_type=F32)


def convolve(hi, lo, taps, f1, f2, g, tw):
    n, rows = hi.shape
    g_hi, g_lo = g[0], g[1]
    cos, sin = tw[0], tw[1]

    def within(re, im):
        high, low = halves(jnp.concatenate([re, im], 1))
        return mm(high, g_hi) + (mm(low, g_hi) + mm(high, g_lo))

    both = jnp.concatenate([hi, taps], 1)
    first = mm(f1[0], both) + mm(f1[1], both)
    sig = first[:, :rows] + mm(f1[0], lo)
    ker = first[:, rows:]

    def turned(re, im):
        return re * cos + im * sin, im * cos - re * sin

    s_re, s_im = turned(sig[:n], sig[n:])
    k_re, k_im = turned(ker[:n], ker[n:])
    spec = within(jnp.concatenate([s_re, k_re], 0), jnp.concatenate([s_im, k_im], 0))
    s_re, s_im = spec[:n, :rows], spec[:n, rows:]
    k_re, k_im = spec[n:, :rows], spec[n:, rows:]
    p_re = s_re * k_re - s_im * k_im
    p_im = -(s_re * k_im + s_im * k_re)
    back = within(p_re, p_im)
    w_re, w_im = turned(back[:, :rows], back[:, rows:])
    high, low = halves(jnp.concatenate([w_re, w_im], 0))
    out = mm(f2[0], jnp.concatenate([high, low], 1))
    return out[:, :rows] + (out[:, rows:] + mm(f2[1], high))


def kernel(
    inner_hbm, value_hbm, outer_hbm, taps_hbm, w_hbm, f1_hbm, f2_hbm, g_hbm, tw_hbm, f1f_hbm, f2f_hbm, twf_hbm, own0_hbm, own1_hbm, far_hbm,
    inner_ref, value_ref, outer_ref, taps_ref, send, send_o, got, got_o, got_f, got_fo, send_g, send_gf, got_g, w, wxa, wxb, f1, f2, g, tw, f1f, f2f, twf, mine, gx, acc0, acc1, s1, r1, s2, r2, zs, own,
    load_sem, own_sem, far_sem, a_ss, a_rs, b_ss, b_rs, p_ss, p_rs, o_ss, o_rs, g_ss, g_rs, h_ss, h_rs, wa_ss, wa_rs, wb_ss, wb_rs, f_ss, f_rs, gx_ss, gx_rs, s1_ss, s1_rs, s2_ss, s2_rs, z_ss, z_rs,
):
    seq = lax.axis_size("seq")
    me, chan = lax.axis_index("seq"), lax.axis_index("chan")
    x, zh, y = lax.div(chan, NZ * NY), lax.rem(lax.div(chan, NY), NZ), lax.rem(chan, NY)
    xs = [x] + [lax.rem(x + d, NX) for d in range(1, NX)]
    ys = [y] + [lax.rem(y + d, NY) for d in range(1, NY)]
    zs_of = [zh, 1 - zh]
    flips = [(1 << b) * (1 - 2 * lax.rem(lax.div(me, 1 << b), 2)) for b in range(seq.bit_length() - 1)]

    def flipped(bits):
        return sum((flip for b, flip in enumerate(flips) if bits >> b & 1), me)
    half, channels = own0_hbm.shape
    rows = 2 * half
    group = channels // seq

    def at(dx, dz, dy):
        return (xs[dx] * NZ + zs_of[dz]) * NY + ys[dy]

    others = [(flipped(k), chan) for k in reversed(range(1, seq))]
    others += [(me, at(d, 0, 0)) for d in range(1, NX)] + [(me, at(0, 0, d)) for d in range(1, NY)]
    barrier = pltpu.get_barrier_semaphore()
    for other in others:
        pl.semaphore_signal(barrier, inc=1, device_id=other, device_id_type=MESH)
    far = (me, at(0, 1, 0))

    @pl.when(zh == 0)
    def _():
        pl.semaphore_signal(barrier, inc=1, device_id=far, device_id_type=MESH)

    pairs = [
        (inner_hbm, inner_ref), (value_hbm, value_ref), (taps_hbm, taps_ref), (outer_hbm, outer_ref),
        (f1_hbm, f1), (f2_hbm, f2), (g_hbm, g), (tw_hbm, tw), (w_hbm, w),
        (f1f_hbm, f1f), (f2f_hbm, f2f), (twf_hbm, twf),
    ]
    loads = [pltpu.make_async_copy(src, dst, load_sem.at[i]) for i, (src, dst) in enumerate(pairs)]
    for load in loads:
        load.start()

    loads[0].wait()
    loads[1].wait()
    signal = (inner_ref[...].astype(F32) * value_ref[...].astype(F32)).T
    hi, lo = halves(signal)
    send[:, 0:group] = hi.reshape(seq, group, rows)
    send[:, group : 2 * group] = lo.reshape(seq, group, rows)
    loads[2].wait()
    send[:, 2 * group : 3 * group] = taps_ref[...].astype(F32).T.astype(BF16).reshape(seq, group, rows)
    loads[3].wait()
    send_o[...] = outer_ref[...].astype(F32).T.astype(BF16).reshape(seq, group, rows)
    pl.semaphore_wait(barrier, len(others) + zh)

    @pl.when(zh == 1)
    def _():
        pl.semaphore_signal(far_sem, inc=1, device_id=far, device_id_type=MESH)

    def remote(src, dst, ss, rs, dx=0, dz=0, dy=0, to=None):
        copy = pltpu.make_async_remote_copy(
            src_ref=src, dst_ref=dst, send_sem=ss, recv_sem=rs,
            device_id=(me, at(dx, dz, dy)) if to is None else to, device_id_type=MESH,
        )
        copy.start()
        return copy

    mid = seq // 2
    first, second_half = me < mid, me >= mid

    def block_of(device):
        return 2 * lax.rem(device, mid) + lax.div(device, mid)


    def to_first(k, gates=False):
        to = flipped(k)
        src, dst, ss, rs = (send_o, got_fo, p_ss, p_rs) if gates else (send, got_f, b_ss, b_rs)
        return pltpu.make_async_remote_copy(
            src_ref=src.at[pl.ds(2 * to, 2)], dst_ref=dst.at[me], send_sem=ss.at[k - 1], recv_sem=rs.at[k - 1],
            device_id=(to, chan), device_id_type=MESH,
        )

    @pl.when(first)
    def _():
        for k in reversed(range(1, mid)):
            to_first(k).start()
        got_f[me] = send[pl.ds(2 * me, 2)]
        got_fo[me] = send_o[pl.ds(2 * me, 2)]

    def full_to(k):
        to = flipped(k)
        return pltpu.make_async_remote_copy(
            src_ref=send.at[block_of(to)], dst_ref=got.at[me], send_sem=a_ss.at[k - 1], recv_sem=a_rs.at[k - 1],
            device_id=(to, chan), device_id_type=MESH,
        )

    def outer_to(k):
        to = flipped(k)
        return pltpu.make_async_remote_copy(
            src_ref=send_o.at[block_of(to)], dst_ref=got_o.at[me - mid], send_sem=o_ss.at[k - 1], recv_sem=o_rs.at[me - mid],
            device_id=(to, chan), device_id_type=MESH,
        )

    across, near = list(reversed(range(mid, seq))), list(reversed(range(1, mid)))
    for k in across:
        full_to(k).start()

    @pl.when(first)
    def _():
        for k in near:
            to_first(k, True).start()

    @pl.when(second_half)
    def _():
        for k in near:
            full_to(k).start()
        for k in across + near:
            outer_to(k).start()
        got[me] = send[block_of(me)]
        got_o[me - mid] = send_o[block_of(me)]

    def outer_from(i):
        return pltpu.make_async_remote_copy(
            src_ref=send_o.at[i], dst_ref=got_o.at[i], send_sem=o_ss.at[i], recv_sem=o_rs.at[i],
            device_id=(mid + i, chan), device_id_type=MESH,
        )

    order, width = [2, 1, 3, 0], channels
    core = lax.rem(me, 2)
    sibling = (me + 1 - 2 * core, chan)
    part = pl.ds(pl.multiple_of(core * (channels // 2), channels // 2), channels // 2)
    weights, onward = {}, []

    def pass_on(d):
        weights[0, d].wait_recv()
        onward.append(remote(wxa.at[d - 1, part], wxa.at[d - 1, part], f_ss.at[0, d - 1], f_rs.at[0, d - 1], to=sibling))
        for i in range(NX):
            weights[1, d, i].wait_recv()
        onward.append(remote(wxb.at[d - 1, :, part], wxb.at[d - 1, :, part], f_ss.at[1, d - 1], f_rs.at[1, d - 1], to=sibling))

    loads[8].wait()
    for d in (1, 3, 2):
        column = pl.multiple_of((xs[d] * NZ + 1 - zh) * NY * width, NY * width)
        weights[0, d] = remote(
            w.at[part, pl.ds(column, NY * width)], wxa.at[d - 1, part], wa_ss.at[d - 1], wa_rs.at[d - 1], dx=d
        )
        for i in range(NX):
            column = pl.multiple_of(((i * NZ + 1 - zh) * NY + ys[d]) * width, width)
            weights[1, d, i] = remote(
                w.at[part, pl.ds(column, width)], wxb.at[d - 1, i, part], wb_ss.at[d - 1, i], wb_rs.at[d - 1, i], dy=d
            )
    for load in loads[4:8] + loads[9:]:
        load.wait()
    n = seq * group

    def back_first(to, source):
        return pltpu.make_async_remote_copy(
            src_ref=send_gf.at[to], dst_ref=got_g.at[pl.ds(2 * source, 2)], send_sem=h_ss.at[to], recv_sem=h_rs.at[source],
            device_id=(to, chan), device_id_type=MESH,
        )

    def back_second(i, source):
        return pltpu.make_async_remote_copy(
            src_ref=send_g.at[i], dst_ref=got_g.at[block_of(source)], send_sem=g_ss.at[i], recv_sem=g_rs.at[source],
            device_id=(mid + i, chan), device_id_type=MESH,
        )

    @pl.when(first)
    def _():
        for k in range(1, mid):
            to_first(k).wait_recv()
        conv = convolve(
            got_f[:, :, 0:group].reshape(n, rows), got_f[:, :, group : 2 * group].reshape(n, rows),
            got_f[:, :, 2 * group : 3 * group].reshape(n, rows), f1f, f2f, g, twf,
        )
        for k in range(1, mid):
            to_first(k, True).wait_recv()
        gated = (got_fo[...].reshape(n, rows).astype(F32) * conv).astype(BF16)
        send_gf[...] = gated.reshape(mid, 2, group, rows)
        for i in range(mid - 1):
            back_first(i + (i >= me).astype(jnp.int32), me).start()
        got[:mid] = got_f[:, 0]
        got_g[pl.ds(2 * me, 2)] = send_gf[me]

    pass_on(1)
    pass_on(3)
    for k in across:
        full_to(k).wait_recv()

    @pl.when(second_half)
    def _():
        for k in near:
            full_to(k).wait_recv()

    conv = convolve(
        got[:, 0:group].reshape(n, rows), got[:, group : 2 * group].reshape(n, rows),
        got[:, 2 * group : 3 * group].reshape(n, rows), f1, f2, g, tw,
    )
    for i in range(mid):

        @pl.when(me != mid + i)
        def _():
            outer_from(i).wait_recv()

    gated = (got_o[...].reshape(n // 2, rows).astype(F32) * conv).astype(BF16)
    send_g[...] = gated.reshape(mid, group, rows)
    for i in range(mid):

        @pl.when(me != mid + i)
        def _():
            back_second(i, me).start()

    @pl.when(second_half)
    def _():
        got_g[block_of(me)] = send_g[me - mid]

    pass_on(2)

    @pl.when(first)
    def _():
        for k in range(1, mid):
            back_first(me, flipped(k)).wait_recv()

    @pl.when(second_half)
    def _():
        for k in range(1, seq):
            back_second(me - mid, flipped(k)).wait_recv()

    mine[...] = got_g[...].reshape(n, rows).astype(F32).T.astype(BF16)

    gather, stage1, stage2, last = {}, {}, {}, []
    for d in order[:3]:
        for h in range(2):
            gather[h, d] = remote(
                mine.at[pl.ds(h * half, half)], gx.at[h, d - 1], gx_ss.at[h, d - 1], gx_rs.at[h, d - 1],
                d * (1 - h), 0, d * h,
            )
    for i in range(4):
        for h in range(2):
            block = (x * NZ + 1 - zh) * NY + i if h == 0 else (i * NZ + 1 - zh) * NY + y
            column = pl.multiple_of(block * width, width)
            acc0[h, i] = mm(mine[h * half : (h + 1) * half], w[:, pl.ds(column, width)])
    for dx in order:
        for dy in order:
            column = pl.multiple_of(at(dx, 0, dy) * width, width)
            block = mm(mine[...], w[:, pl.ds(column, width)])
            if dx == 0:
                acc1[0, dy] = block[:half]
            else:
                s1[0, dx - 1, :, dy * width : (dy + 1) * width] = block[:half].astype(BF16)
            if dy == 0:
                acc1[1, dx] = block[half:]
            else:
                s1[1, dy - 1, :, dx * width : (dx + 1) * width] = block[half:].astype(BF16)
    for d in order[:1]:
        for h in range(2):
            stage1[h, d] = remote(
                s1.at[h, d - 1], r1.at[h, d - 1], s1_ss.at[h, d - 1], s1_rs.at[h, d - 1], d * (1 - h), 0, d * h
            )
    for copy in onward:
        copy.wait_recv()
    for d in (1, 3, 2):
        for h in range(2):
            gather[h, d].wait_recv()
            for i in range(4):
                block = wxa[d - 1, :, i * width : (i + 1) * width] if h == 0 else wxb[d - 1, i]
                acc0[h, i] += mm(gx[h, d - 1], block)

    def second(wave, h, d, total):
        s2[wave, h, d - 1] = total.astype(BF16)
        stage2[wave, h, d] = remote(
            s2.at[wave, h, d - 1], r2.at[wave, h, d - 1], s2_ss.at[wave, h, d - 1], s2_rs.at[wave, h, d - 1],
            d * h, 0, d * (1 - h),
        )

    def finished(wave, h, total):
        for d in (1, 3, 2):
            stage2[wave, h, d].wait_recv()
            total = total + r2[wave, h, d - 1].astype(F32)
        return total

    for d in order[:3]:
        for h in range(2):
            second(0, h, d, acc0[h, ys[d] if h == 0 else xs[d]])
    for d in order[1:3]:
        for h in range(2):
            stage1[h, d] = remote(
                s1.at[h, d - 1], r1.at[h, d - 1], s1_ss.at[h, d - 1], s1_rs.at[h, d - 1], d * (1 - h), 0, d * h
            )
    @pl.when(first)
    def _():
        for k in range(1, mid):
            to_first(k).wait_send()
            to_first(k, True).wait_send()
        for i in range(mid - 1):
            back_first(i + (i >= me).astype(jnp.int32), me).wait_send()

    @pl.when(second_half)
    def _():
        for k in across + near:
            outer_to(k).wait_send()
        for k in near:
            full_to(k).wait_send()

    for k in across:
        full_to(k).wait_send()

    for i in range(mid):

        @pl.when(me != mid + i)
        def _():
            back_second(i, me).wait_send()
    for copy in onward + list(weights.values()) + list(gather.values()):
        copy.wait_send()
    for h in range(2):
        total = finished(0, h, acc0[h, y if h == 0 else x])
        if h == 0:

            @pl.when(zh == 0)
            def _():
                pl.semaphore_wait(far_sem, 1)

        zs[h] = total.astype(BF16)
        last.append(remote(zs.at[h], far_hbm.at[h], z_ss.at[h], z_rs.at[h], 0, 1, 0))
    for h in range(2):
        for d in (1, 3, 2):
            stage1[h, d].wait_recv()
        for d in order:
            total = acc1[h, d]
            for e in range(3):
                total = total + r1[h, e, :, d * width : (d + 1) * width].astype(F32)
            if d:
                second(1, h, d, total)
            else:
                acc1[h, 0] = total
    stores = []
    for h in range(2):
        own[h] = finished(1, h, acc1[h, 0])
        stores.append(pltpu.make_async_copy(own.at[h], (own0_hbm, own1_hbm)[h], own_sem.at[h]))
        stores[h].start()
    for copy in list(stage1.values()) + list(stage2.values()):
        copy.wait_send()
    for copy in last:
        copy.wait_recv()
    for store in stores:
        store.wait()
    for copy in last:
        copy.wait_send()


def local(inner_gate, value_in, outer_gate, filter_taps, out_weight):
    rows, channels = inner_gate.shape
    seq = lax.axis_size("seq")
    group, half = channels // seq, rows // 2
    f1, f2, g, tw = transform_constants(seq, rows, group)
    f2 = f2[:, f2.shape[1] // 2 :]
    f1f, f2f, _, twf = transform_constants(seq // 2, rows, 2 * group)
    vmem, dma = pltpu.VMEM, pltpu.SemaphoreType.DMA
    in_hbm, in_any = pl.BlockSpec(memory_space=pltpu.HBM), pl.BlockSpec(memory_space=pl.ANY)
    peers, mid = seq - 1, seq // 2
    scratch = [
        *[vmem((rows, channels), BF16)] * 4,
        vmem((seq, 3 * group, rows), BF16), vmem((seq, group, rows), BF16),
        vmem((seq, 3 * group, rows), BF16), vmem((mid, group, rows), BF16),
        vmem((mid, 2, 3 * group, rows), BF16), vmem((mid, 2, group, rows), BF16),
        vmem((mid, group, rows), BF16), vmem((mid, 2, group, rows), BF16), vmem((seq, group, rows), BF16),
        vmem(out_weight.shape, BF16), vmem((3, channels, NY * channels), BF16), vmem((3, NX, channels, channels), BF16),
        vmem(f1.shape, BF16), vmem(f2.shape, BF16), vmem(g.shape, BF16), vmem(tw.shape, F32),
        vmem(f1f.shape, BF16), vmem(f2f.shape, BF16), vmem(twf.shape, F32),
        vmem((rows, channels), BF16), vmem((2, 3, half, channels), BF16),
        vmem((2, 4, half, channels), F32), vmem((2, 4, half, channels), F32),
        vmem((2, 3, half, 4 * channels), BF16), vmem((2, 3, half, 4 * channels), BF16),
        vmem((2, 2, 3, half, channels), BF16), vmem((2, 2, 3, half, channels), BF16),
        vmem((2, half, channels), BF16), vmem((2, half, channels), F32),
        dma((12,)), dma((2,)), pltpu.SemaphoreType.REGULAR, dma((peers,)), dma((peers,)), *[dma((mid - 1,))] * 4, dma((peers,)), dma((mid,)),
        dma((mid,)), dma((seq,)), dma((mid,)), dma((mid,)),
        dma((3,)), dma((3,)), dma((3, 4)), dma((3, 4)), dma((2, 3)), dma((2, 3)), dma((2, 3)), dma((2, 3)),
        dma((2, 3)), dma((2, 3)), dma((2, 2, 3)), dma((2, 2, 3)), dma((2,)), dma((2,)),
    ]
    *own, far = pl.pallas_call(
        kernel,
        out_shape=(*[jax.ShapeDtypeStruct((half, channels), F32)] * 2, jax.ShapeDtypeStruct((2, half, channels), BF16)),
        in_specs=[in_hbm] * 12,
        out_specs=(in_any,) * 3,
        scratch_shapes=scratch,
        compiler_params=pltpu.CompilerParams(collective_id=0, has_side_effects=True, vmem_limit_bytes=5372 * 2**20 // 100),
        name="hyena",
    )(inner_gate, value_in, outer_gate, filter_taps, out_weight, *(jnp.asarray(c) for c in (f1, f2, g, tw, f1f, f2f, twf)))
    return jnp.concatenate([part + far[h].astype(F32) for h, part in enumerate(own)], 0)


def solution(mesh):
    in_specs = (P("seq", "chan"),) * 4 + (P("chan", None),)
    return jax.shard_map(local, mesh=mesh, in_specs=in_specs, out_specs=P("seq", "chan"), check_vma=False)
```
